32 devices in a mesh: gx: 4 (over y, core), gy: 4 (over z), gz: 2 (over x).
Axes of the slice: x: 2, y: 2, z: 4, core: 2. Of those that a mesh axis runs over, the one named last changes fastest.
Arguments:
- particles: bfloat16 [4, 4, 2, 256, 512], P('gx', 'gy', 'gz'), may hold values from -6 to 6
- log_weight: bfloat16 [4, 4, 2, 256], P('gx', 'gy', 'gz'), may hold values from -4 to 296
- counts: int32 [4, 4, 2], P('gx', 'gy', 'gz'), may hold values from 1 to 256, as said below
- pattern: int32 [4, 4, 2, 6], P('gx', 'gy', 'gz'), may hold values from 0 to 1, as said below
- query_weight: bfloat16 [512, 512], replicated, may hold values from -0.25 to 0.25
- key_value_weight: bfloat16 [512, 1024], replicated, may hold values from -0.25 to 0.25
- output_weight: bfloat16 [512, 512], replicated, may hold values from -0.75 to 0.75
- baffle_store: bfloat16 [32, 1024, 1024], P(('gx', 'gy', 'gz')), may hold values from -6 to 6
- owner_device: int32 [1], replicated, may hold values from 0 to 31
- cotangent: bfloat16 [4, 4, 2, 256, 512], P('gx', 'gy', 'gz'), may hold values from -6 to 6
Outputs:
- update: bfloat16 [4, 4, 2, 256, 512], P('gx', 'gy', 'gz')
- grad_particles: bfloat16 [4, 4, 2, 256, 512], P('gx', 'gy', 'gz')
- grad_query: float32 [262144], P(('gx', 'gy', 'gz'))
- grad_key_value: float32 [524288], P(('gx', 'gy', 'gz'))
- grad_output: float32 [262144], P(('gx', 'gy', 'gz'))
- grad_baffle: float32 [1048576], P(('gx', 'gy', 'gz'))
The draws below stay inside these ranges and needn't reach their ends.
Inputs may be any that keep to these rules, and one draw needn't show every extreme that they name: A patch holds its particles in its first counts slots. Patches whose z index lies below a drawn fill level hold 256 particles; the bottom layer always lies below it and the top layer never; the others hold 1 to 256. `pattern`: entries 2k and 2k+1 flag the lower and upper neighbour along grid dimension k (x, y, z). A flag is 0 where that neighbour lies outside the grid, and a patch flags a neighbour exactly when that neighbour flags it back. `owner_device`: the index of the device along gx+gy+gz, slowest axis first.
All inputs are finite; a program needn't handle non-finite values.
Results may differ from the reference program's by a relative error of at most 0.012.
The reference program's roundings to bfloat16 on the way count: a program that leaves them out, or rounds other values in their place, can miss the bound.
Values may be sent and summed in bfloat16 or wider, within the bound.
A program may use at most 128 MiB of HBM per device.

```python
import math
import jax
import jax.numpy as jnp
from jax import lax

D = 512
H = 8
HD = 64
P_SIZE = 256
NB = 1024
GRID_X = 4
GRID_Y = 4
GRID_Z = 2
DEVICES = 32


def draw_log_weight(key, part):
    key = jax.random.fold_in(key, 31)
    base_key = jax.random.fold_in(key, 0)
    grid_shape = (GRID_X, GRID_Y, GRID_Z, P_SIZE)
    values = jnp.clip(jax.random.normal(base_key, grid_shape, jnp.float32), -4.0, 4.0)
    return values.astype(jnp.bfloat16)


def draw_counts(key, part):
    key = jax.random.fold_in(key, 32)
    level_key, fill_key = jax.random.split(key)
    grid_shape = (GRID_X, GRID_Y, GRID_Z)
    surface = jax.random.randint(level_key, (), 1, GRID_Z)
    partial_fill = jax.random.randint(fill_key, grid_shape, 1, P_SIZE + 1)
    layer_index = lax.broadcasted_iota(jnp.int32, grid_shape, 2)
    return jnp.where(layer_index < surface, P_SIZE, partial_fill).astype(jnp.int32)


def open_faces(sub_key, extent_shape, axis_index):
    opened = jax.random.randint(sub_key, extent_shape, 0, 8) < 7
    position = lax.broadcasted_iota(jnp.int32, extent_shape, axis_index)
    inside = (position > 0) & (position < extent_shape[axis_index] - 1)
    return (opened & inside).astype(jnp.int32)


def draw_pattern(key, part):
    key = jax.random.fold_in(key, 33)
    split_keys = jax.random.split(key, 3)
    face_x = open_faces(split_keys[0], (GRID_X + 1, GRID_Y, GRID_Z), 0)
    face_y = open_faces(split_keys[1], (GRID_X, GRID_Y + 1, GRID_Z), 1)
    face_z = open_faces(split_keys[2], (GRID_X, GRID_Y, GRID_Z + 1), 2)
    return jnp.stack([face_x[:-1], face_x[1:], face_y[:, :-1], face_y[:, 1:], face_z[:, :, :-1], face_z[:, :, 1:]], axis=3).astype(jnp.int32)


def shard_levels(rng, extent, shards, low, largest):
    def one(axis_at, shards_of):
        draws = jax.random.uniform(jax.random.fold_in(jax.random.fold_in(rng, 6), axis_at), (shards_of,), jnp.float32, low / len(shards), largest / len(shards))
        return jnp.repeat(jnp.exp(draws), extent[axis_at] // shards_of).reshape((-1,) + (1,) * (len(extent) - axis_at - 1))

    gain = one(*shards[0])
    for cut in shards[1:]:
        gain = gain * one(*cut)
    return gain


def centred(stream_key, extent, width, limit, cuts=(), kind=jnp.bfloat16):
    level = shard_levels(stream_key, extent, cuts, -0.22, 0.18) if cuts else 1.0
    entries = jax.random.normal(stream_key, extent, jnp.float32) * width * level
    return jnp.minimum(jnp.maximum(entries, -limit), limit).astype(kind)


def setup_inputs(seed: int = 0) -> dict:
    streams_of = jax.random.split(jax.random.key(seed), 11)
    return {
        "particles": centred(streams_of[0], (GRID_X, GRID_Y, GRID_Z, P_SIZE, D), 1.0, 6.0, ((0, 4), (1, 4), (2, 2))),
        "log_weight": draw_log_weight(jax.random.fold_in(streams_of[10], 71), 0),
        "counts": draw_counts(jax.random.fold_in(streams_of[10], 71), 0),
        "pattern": draw_pattern(jax.random.fold_in(streams_of[10], 71), 0),
        "query_weight": centred(streams_of[4], (D, D), D ** -0.5, 0.25),
        "key_value_weight": centred(streams_of[5], (D, 2 * D), D ** -0.5, 0.25),
        "output_weight": centred(streams_of[6], (D, D), HD ** -0.5, 0.75),
        "baffle_store": centred(streams_of[7], (DEVICES, NB, 2 * D), 1.0, 6.0, ((0, 32),)),
        "owner_device": jax.random.randint(streams_of[8], (1,), 0, DEVICES).astype(jnp.int32),
        "cotangent": centred(streams_of[9], (GRID_X, GRID_Y, GRID_Z, P_SIZE, D), 1.0, 6.0, ((0, 4), (1, 4), (2, 2))),
    }


masked_bias = -1000000000.0

def layer_norm(values):
    row_mean = lax.optimization_barrier(jnp.mean(values, axis=-1, keepdims=True))
    centered = values - row_mean
    inv_std = lax.rsqrt(lax.optimization_barrier(jnp.mean(centered * centered, axis=-1, keepdims=True)) + 1e-05)
    return (centered * inv_std, inv_std)

def layer_norm_back(grad_normed, normed, inv_std):
    first_mean = lax.optimization_barrier(jnp.mean(grad_normed, axis=-1, keepdims=True))
    second_mean = lax.optimization_barrier(jnp.mean(grad_normed * normed, axis=-1, keepdims=True))
    return inv_std * (grad_normed - first_mean - normed * second_mean)

def contract_last(left, right):
    return lax.dot_general(left, right, (((1,), (1,)), ((), ())), preferred_element_type=jnp.float32)

def contract_first(left, right):
    return lax.dot_general(left, right, (((0,), (0,)), ((), ())), preferred_element_type=jnp.float32)

def head_columns(block, head_index, offset):
    return lax.dynamic_slice_in_dim(block, offset + head_index * HD, HD, 1)

def merge_heads(stacked):
    return jnp.transpose(stacked, (1, 0, 2)).reshape(stacked.shape[1], stacked.shape[0] * stacked.shape[2])

def attend_forward(queries, all_keys, key_bias):
    score_scale = 1.0 / math.sqrt(HD)

    def per_head(head_index):
        query_head = head_columns(queries, head_index, 0)
        key_head = head_columns(all_keys, head_index, 0)
        value_head = head_columns(all_keys, head_index, D)
        scores = contract_last(query_head, key_head) * score_scale + key_bias[None, :]
        top_score = lax.optimization_barrier(jnp.max(scores, axis=1, keepdims=True))
        log_total = top_score[:, 0] + jnp.log(lax.optimization_barrier(jnp.sum(jnp.exp(scores - top_score), axis=1)))
        prob_low = jnp.exp(scores - log_total[:, None]).astype(jnp.bfloat16)
        return (jnp.dot(prob_low, value_head, preferred_element_type=jnp.float32), log_total)
    head_out, log_totals = lax.map(per_head, jnp.arange(H, dtype=jnp.int32))
    return (merge_heads(head_out).astype(jnp.bfloat16), log_totals)

def query_back(queries, all_keys, key_bias, log_totals, attn, grad_attn):
    score_scale = 1.0 / math.sqrt(HD)
    baffle_start = all_keys.shape[0] - NB

    def per_head(head_index):
        query_head = head_columns(queries, head_index, 0)
        key_head = head_columns(all_keys, head_index, 0)
        value_head = head_columns(all_keys, head_index, D)
        attn_head = head_columns(attn, head_index, 0)
        grad_head = head_columns(grad_attn, head_index, 0)
        scores = contract_last(query_head, key_head) * score_scale + key_bias[None, :]
        prob_full = jnp.exp(scores - log_totals[head_index][:, None])
        prob_low = prob_full.astype(jnp.bfloat16)
        row_dot = lax.optimization_barrier(jnp.sum(grad_head.astype(jnp.float32) * attn_head.astype(jnp.float32), axis=1))
        grad_prob = contract_last(grad_head, value_head)
        grad_score = (prob_full * (grad_prob - row_dot[:, None])).astype(jnp.bfloat16)
        grad_query_head = jnp.dot(grad_score, key_head, preferred_element_type=jnp.float32) * score_scale
        grad_bkey = contract_first(grad_score[:, baffle_start:], query_head) * score_scale
        grad_bvalue = contract_first(prob_low[:, baffle_start:], grad_head)
        return (grad_query_head, row_dot, grad_bkey, grad_bvalue)
    grad_heads, row_dots, bkey_heads, bvalue_heads = lax.map(per_head, jnp.arange(H, dtype=jnp.int32))
    baffle_grad = jnp.concatenate([merge_heads(bkey_heads), merge_heads(bvalue_heads)], axis=1)
    return (merge_heads(grad_heads).astype(jnp.bfloat16), row_dots, baffle_grad)

def key_back(query_rows, grad_rows, total_rows, dot_rows, keep_rows, own_pairs, own_bias):
    score_scale = 1.0 / math.sqrt(HD)

    def per_head(head_index):
        query_head = head_columns(query_rows, head_index, 0)
        grad_head = head_columns(grad_rows, head_index, 0)
        key_head = head_columns(own_pairs, head_index, 0)
        value_head = head_columns(own_pairs, head_index, D)
        scores = contract_last(query_head, key_head) * score_scale + own_bias[None, :]
        shifted = jnp.where(keep_rows[:, None], scores - total_rows[head_index][:, None], masked_bias)
        prob_full = jnp.exp(shifted)
        grad_prob = contract_last(grad_head, value_head)
        grad_score = (prob_full * (grad_prob - dot_rows[head_index][:, None])).astype(jnp.bfloat16)
        grad_key_head = contract_first(grad_score, query_head) * score_scale
        grad_value_head = contract_first(prob_full.astype(jnp.bfloat16), grad_head)
        return (grad_key_head, grad_value_head)
    key_heads, value_heads = lax.map(per_head, jnp.arange(H, dtype=jnp.int32))
    return jnp.concatenate([merge_heads(key_heads), merge_heads(value_heads)], axis=1).astype(jnp.bfloat16)

def neighbour_table():
    flat_index = jnp.arange(GRID_X * GRID_Y * GRID_Z, dtype=jnp.int32)
    pos_x = flat_index // (GRID_Y * GRID_Z)
    pos_y = flat_index // GRID_Z % GRID_Y
    pos_z = flat_index % GRID_Z

    def linear(along_x, along_y, along_z):
        along_x = jnp.clip(along_x, 0, GRID_X - 1)
        along_y = jnp.clip(along_y, 0, GRID_Y - 1)
        along_z = jnp.clip(along_z, 0, GRID_Z - 1)
        return ((along_x * GRID_Y + along_y) * GRID_Z + along_z).astype(jnp.int32)
    return jnp.stack([linear(pos_x - 1, pos_y, pos_z), linear(pos_x + 1, pos_y, pos_z), linear(pos_x, pos_y - 1, pos_z), linear(pos_x, pos_y + 1, pos_z), linear(pos_x, pos_y, pos_z - 1), linear(pos_x, pos_y, pos_z + 1)], axis=1)

def reference(particles, log_weight, counts, pattern, query_weight, key_value_weight, output_weight, baffle_store, owner_device, cotangent):
    patches = GRID_X * GRID_Y * GRID_Z
    flat_rows = particles.reshape(patches * P_SIZE, D).astype(jnp.float32)
    normed, inv_std = layer_norm(flat_rows)
    normed_low = normed.astype(jnp.bfloat16)
    queries = jnp.dot(normed_low, query_weight, preferred_element_type=jnp.float32).astype(jnp.bfloat16).reshape(patches, P_SIZE, D)
    key_value = jnp.dot(normed_low, key_value_weight, preferred_element_type=jnp.float32).astype(jnp.bfloat16).reshape(patches, P_SIZE, 2 * D)
    slot_index = jnp.arange(P_SIZE, dtype=jnp.int32)
    valid_rows = slot_index[None, :] < counts.reshape(patches)[:, None]
    own_bias = jnp.where(valid_rows, log_weight.reshape(patches, P_SIZE), jnp.asarray(masked_bias, jnp.bfloat16))
    face_flags = pattern.reshape(patches, 6) == 1
    neighbours = neighbour_table()
    baffle = lax.dynamic_index_in_dim(baffle_store, owner_device[0], 0, keepdims=False)
    zero_bias = jnp.zeros((NB,), jnp.float32)
    grad_inputs = jnp.where(valid_rows[:, :, None], cotangent.reshape(patches, P_SIZE, D), jnp.zeros((), jnp.bfloat16))

    def forward_step(carry, patch):
        nearby = neighbours[patch]
        pairs = jnp.concatenate([key_value[patch][None], key_value[nearby]], axis=0).reshape(7 * P_SIZE, 2 * D)
        all_keys = jnp.concatenate([pairs, baffle], axis=0)
        nearby_bias = jnp.where(face_flags[patch][:, None], own_bias[nearby].astype(jnp.float32), masked_bias)
        key_bias = jnp.concatenate([own_bias[patch].astype(jnp.float32), nearby_bias.reshape(6 * P_SIZE), zero_bias])
        attn, log_totals = attend_forward(queries[patch], all_keys, key_bias)
        projected = jnp.dot(attn, output_weight, preferred_element_type=jnp.float32)
        update = jnp.where(valid_rows[patch][:, None], projected, 0.0).astype(jnp.bfloat16)
        grad_attn = contract_last(grad_inputs[patch], output_weight).astype(jnp.bfloat16)
        grad_q, row_dots, baffle_grad = query_back(queries[patch], all_keys, key_bias, log_totals, attn, grad_attn)
        return (carry + baffle_grad, (update, attn, grad_attn, grad_q, log_totals, row_dots))
    baffle_total, stacked = lax.scan(forward_step, jnp.zeros((NB, 2 * D), jnp.float32), jnp.arange(patches, dtype=jnp.int32))
    updates, attns, grad_attns, grad_qs, totals, row_dots_all = stacked

    def key_step(patch):
        members = jnp.concatenate([patch[None], neighbours[patch]])
        keep = jnp.concatenate([jnp.ones((1,), bool), face_flags[patch]])
        keep_rows = jnp.repeat(keep, P_SIZE)
        query_rows = queries[members].reshape(7 * P_SIZE, D)
        grad_rows = grad_attns[members].reshape(7 * P_SIZE, D)
        total_rows = jnp.transpose(totals[members], (1, 0, 2)).reshape(H, 7 * P_SIZE)
        dot_rows = jnp.transpose(row_dots_all[members], (1, 0, 2)).reshape(H, 7 * P_SIZE)
        return key_back(query_rows, grad_rows, total_rows, dot_rows, keep_rows, key_value[patch], own_bias[patch].astype(jnp.float32))
    grad_pairs = lax.map(key_step, jnp.arange(patches, dtype=jnp.int32))
    grad_q_flat = grad_qs.reshape(patches * P_SIZE, D)
    grad_pair_flat = grad_pairs.reshape(patches * P_SIZE, 2 * D)
    grad_normed = contract_last(grad_q_flat, query_weight) + contract_last(grad_pair_flat, key_value_weight)
    grad_flat = layer_norm_back(grad_normed, normed, inv_std).astype(jnp.bfloat16)
    grad_query = contract_first(normed_low, grad_q_flat).reshape(-1)
    grad_key_value = contract_first(normed_low, grad_pair_flat).reshape(-1)
    grad_output = contract_first(attns.reshape(patches * P_SIZE, D), grad_inputs.reshape(patches * P_SIZE, D)).reshape(-1)
    grid_shape = (GRID_X, GRID_Y, GRID_Z, P_SIZE, D)
    return (updates.reshape(grid_shape), grad_flat.reshape(grid_shape), grad_query, grad_key_value, grad_output, baffle_total.reshape(-1))
```

```python
import functools
import math

import jax
import jax.numpy as jnp
from jax import lax
from jax.experimental import pallas as pl
from jax.experimental.pallas import tpu as pltpu
from jax.sharding import PartitionSpec as P

D = 512
H = 8
HD = 64
P_SIZE = 256
NB = 1024
LANES = 128
PAIR = 2 * HD
AUG = 2 * D + LANES
NEAR = 7 * P_SIZE
ALL = NEAR + NB
PIECE = 32

masked_bias = -1000000000.0
F32 = jnp.float32
BF16 = jnp.bfloat16
MESH = pl.DeviceIdType.MESH
VMEM_BYTES = 56 * 1024 * 1024


def nt(left, right):
    return lax.dot_general(left, right, (((1,), (1,)), ((), ())), preferred_element_type=F32)


def tn(left, right):
    return lax.dot_general(left, right, (((0,), (0,)), ((), ())), preferred_element_type=F32)


def nn(left, right):
    return jnp.dot(left, right, preferred_element_type=F32)


def layer_norm(values):
    row_mean = jnp.mean(values, axis=-1, keepdims=True)
    centered = values - row_mean
    inv_std = lax.rsqrt(jnp.mean(centered * centered, axis=-1, keepdims=True) + 1e-05)
    return (centered * inv_std, inv_std)


class Place:
    def __init__(self, sizes):
        self.sizes = sizes
        gx, gy, gz = sizes
        self.at = (lax.axis_index("gx"), lax.axis_index("gy"), lax.axis_index("gz"))
        self.counts = {"y": gx // 2, "c": 2, "gy": gy, "gz": gz}
        self.pos = {
            "y": self.at[0] // 2,
            "c": self.at[0] % 2,
            "gy": self.at[1],
            "gz": self.at[2],
        }

    def device(self, axis, position):
        pos = dict(self.pos)
        pos[axis] = position
        return (pos["y"] * 2 + pos["c"], pos["gy"], pos["gz"])

    def barrier(self):
        sem = pltpu.get_barrier_semaphore()
        total = 0
        for dim, count in enumerate(self.sizes):
            for step in range(1, count):
                target = list(self.at)
                target[dim] = lax.rem(self.at[dim] + step, count)
                pl.semaphore_signal(sem, inc=1, device_id=tuple(target), device_id_type=MESH)
                total += 1
        pl.semaphore_wait(sem, total)

    def faces(self):
        found = []
        for dim, count in enumerate(self.sizes):
            for side in (-1, 1):
                there = self.at[dim] > 0 if side < 0 else self.at[dim] < count - 1
                target = list(self.at)
                target[dim] = jnp.clip(self.at[dim] + side, 0, count - 1)
                found.append((there, tuple(target)))
        return found


AXES = ("y", "c", "gy", "gz")
ORDERS = (("c", "gz", "y", "gy"), ("c", "y", "gz", "gy"))


def select(fixed, rows):
    return tuple(fixed.get(axis, slice(None)) for axis in AXES) + (rows, slice(None))


def stage_plan(sizes):
    gx, gy, gz = sizes
    counts = {"y": gx // 2, "c": 2, "gy": gy, "gz": gz}
    plan = []
    for half, order in enumerate(ORDERS):
        done = []
        for axis in order:
            done.append(axis)
            left = tuple(counts[a] for a in AXES if a not in done)
            plan.append((half, axis, counts[axis], left))
    return counts, plan


def scatter_scratch(sizes, width):
    counts, plan = stage_plan(sizes)
    rows = PIECE // 2
    shapes = [pltpu.VMEM((n - 1,) + left + (rows, width), BF16) for _, _, n, left in plan]
    copies = sum(n - 1 for _, _, n, _ in plan)
    work = pltpu.VMEM((counts["y"], 2, counts["gy"], counts["gz"], PIECE, width), BF16)
    return shapes + [work, pltpu.SemaphoreType.DMA((copies,)), pltpu.SemaphoreType.DMA((copies,))]


class Scatter:
    def __init__(self, place, source, scratch):
        self.place = place
        self.source = source
        self.recv = scratch[:8]
        self.work, self.send_sem, self.recv_sem = scratch[8:11]
        self.plan = stage_plan(place.sizes)[1]
        self.offsets = []
        total = 0
        for _, _, n, _ in self.plan:
            self.offsets.append(total)
            total += n - 1

    def rows(self, half):
        return pl.ds(half * (PIECE // 2), PIECE // 2)

    def fixed(self, half, level):
        return {axis: self.place.pos[axis] for axis in ORDERS[half][:level]}

    def copies(self, half, level):
        at = half * 4 + level
        axis, n = self.plan[at][1], self.plan[at][2]
        origin = self.source if level == 0 else self.work
        found = []
        for step in range(1, n):
            target = lax.rem(self.place.pos[axis] + step, n)
            fixed = self.fixed(half, level)
            fixed[axis] = target
            found.append(
                pltpu.make_async_remote_copy(
                    src_ref=origin.at[select(fixed, self.rows(half))],
                    dst_ref=self.recv[at].at[step - 1],
                    send_sem=self.send_sem.at[self.offsets[at] + step - 1],
                    recv_sem=self.recv_sem.at[self.offsets[at] + step - 1],
                    device_id=self.place.device(axis, target),
                    device_id_type=MESH,
                )
            )
        return found

    def start(self, level):
        for half in range(2):
            for copy in self.copies(half, level):
                copy.start()

    def finish(self, level, out=None):
        for half in range(2):
            at = half * 4 + level
            for copy in self.copies(half, level):
                copy.wait()
            origin = self.source if level == 0 else self.work
            where = select(self.fixed(half, level + 1), self.rows(half))
            total = origin[where].astype(F32)
            for step in range(self.plan[at][2] - 1):
                total = total + self.recv[at][step].astype(F32)
            if out is None:
                self.work[where] = total.astype(BF16)
            else:
                out[self.rows(half), :] = total.astype(out.dtype)


def gather_copies(place, final, send_sem, recv_sem, level):
    counts, plan = stage_plan(place.sizes)
    found = []
    for half in range(2):
        order = ORDERS[half]
        axis = order[level]
        base = sum(n - 1 for h, a, n, _ in plan[: half * 4 + level])
        fixed = {a: place.pos[a] for a in order[: level + 1]}
        view = final.at[select(fixed, pl.ds(half * (PIECE // 2), PIECE // 2))]
        for step in range(1, counts[axis]):
            target = lax.rem(place.pos[axis] + step, counts[axis])
            found.append(
                pltpu.make_async_remote_copy(
                    src_ref=view,
                    dst_ref=view,
                    send_sem=send_sem.at[base + step - 1],
                    recv_sem=recv_sem.at[base + step - 1],
                    device_id=place.device(axis, target),
                    device_id_type=MESH,
                )
            )
    return found


def project_kernel(sizes, rows_ref, bias_ref, wq, wkv, wo, gin, baf, q_out, g_out, keys, final,
                   *scratch):
    scatter_refs, (gs, gr, hs, hr, piece) = scratch[:11], scratch[11:]
    place = Place(sizes)
    place.barrier()
    scatter = Scatter(place, baf, scatter_refs)
    scatter.start(0)
    normed_low = layer_norm(rows_ref[...].astype(F32))[0].astype(BF16)
    keys[0:P_SIZE, 0 : 2 * D] = nn(normed_low, wkv[...]).astype(BF16)
    keys[0:P_SIZE, 2 * D : AUG] = bias_ref[...]
    faces = place.faces()

    def face_copy(face, slot):
        return pltpu.make_async_remote_copy(
            src_ref=keys.at[pl.ds(0, P_SIZE)],
            dst_ref=keys.at[pl.ds((1 + slot) * P_SIZE, P_SIZE)],
            send_sem=hs.at[face],
            recv_sem=hr.at[slot],
            device_id=faces[face][1],
            device_id_type=MESH,
        )

    scatter.finish(0)
    scatter.start(1)
    for face, (there, _) in enumerate(faces):
        @pl.when(there)
        def _(face=face):
            face_copy(face, face ^ 1).start()

        @pl.when(jnp.logical_not(there))
        def _(face=face):
            keys[(1 + face) * P_SIZE : (2 + face) * P_SIZE, :] = jnp.zeros((P_SIZE, AUG), BF16)

    q_out[...] = nn(normed_low, wq[...]).astype(BF16)
    g_out[...] = nt(gin[...], wo[...]).astype(BF16)
    scatter.finish(1)
    scatter.start(2)
    scatter.finish(2)
    scatter.start(3)
    scatter.finish(3, piece)
    final[place.pos["y"], place.pos["c"], place.pos["gy"], place.pos["gz"]] = piece[...]
    for level in (3, 2, 1, 0):
        sent = gather_copies(place, final, gs, gr, level)
        for copy in sent:
            copy.start()
        for copy in sent:
            copy.wait()
    for face, (there, _) in enumerate(faces):
        @pl.when(there)
        def _(face=face):
            face_copy(face, face ^ 1).wait_send()
            face_copy(face, face).wait_recv()


def attend_kernel(flags, q_ref, g_ref, k_ref, v_ref, b_ref, bk_ref, bv_ref,
                  attn_ref, gq_ref, dk_ref, dv_ref, dbk_ref, dbv_ref, e_scr, p_scr, d_scr):
    lane = lax.broadcasted_iota(jnp.int32, (P_SIZE, PAIR), 1)
    zero = jnp.zeros((P_SIZE, PAIR), BF16)
    q = q_ref[...] * jnp.asarray(1.0 / math.sqrt(HD), BF16)
    g = g_ref[...]
    qcat = jnp.concatenate([jnp.where(lane < HD, q, zero), jnp.where(lane < HD, zero, q)], axis=0)
    gcat = jnp.concatenate([jnp.where(lane < HD, g, zero), jnp.where(lane < HD, zero, g)], axis=0)
    first = (lax.broadcasted_iota(jnp.int32, (2 * P_SIZE, LANES), 1) == 0).astype(BF16)
    qaug = jnp.concatenate([qcat, first], axis=1)
    chunks = ALL // P_SIZE

    def part(c):
        if c < 7:
            return slice(c * P_SIZE, (c + 1) * P_SIZE), k_ref, v_ref, dk_ref, dv_ref
        return slice((c - 7) * P_SIZE, (c - 6) * P_SIZE), bk_ref, bv_ref, dbk_ref, dbv_ref

    top = jnp.full((8, 2 * P_SIZE), -3e38, F32)
    for c in range(chunks):
        rows, keys = part(c)[:2]
        if c < 7:
            bias = b_ref[rows, :]
            if c > 0:
                bias = jnp.where(flags[c - 1] == 1, bias, jnp.asarray(masked_bias, BF16))
            scores = nt(jnp.concatenate([keys[rows, :], bias], axis=1), qaug)
        else:
            scores = nt(keys[rows, :], qcat)
        e_scr[c * P_SIZE : (c + 1) * P_SIZE, :] = scores
        top = jnp.maximum(top, jnp.max(scores.reshape(P_SIZE // 8, 8, 2 * P_SIZE), axis=0))
    top = jnp.max(top, axis=0, keepdims=True)
    total = jnp.zeros((8, 2 * P_SIZE), F32)
    for c in range(chunks):
        span = slice(c * P_SIZE, (c + 1) * P_SIZE)
        e = jnp.exp(e_scr[span, :] - top)
        e_scr[span, :] = e
        total = total + jnp.sum(e.reshape(P_SIZE // 8, 8, 2 * P_SIZE), axis=0)
    inverse = 1.0 / jnp.sum(total, axis=0, keepdims=True)
    attn_t = jnp.zeros((PAIR, 2 * P_SIZE), F32)
    for c in range(chunks):
        span = slice(c * P_SIZE, (c + 1) * P_SIZE)
        rows, _, values = part(c)[:3]
        p = (e_scr[span, :] * inverse).astype(BF16)
        p_scr[span, :] = p
        attn_t = attn_t + tn(values[rows, :], p)
    picked = jnp.concatenate([attn_t[:HD, :P_SIZE], attn_t[HD:, P_SIZE:]], axis=0)
    attn_ref[...] = picked.T.astype(BF16)
    product = g.astype(F32).T * picked.astype(BF16).astype(F32)
    row_dot = jnp.concatenate(
        [
            jnp.sum(product[:HD], axis=0, keepdims=True),
            jnp.sum(product[HD:], axis=0, keepdims=True),
        ],
        axis=1,
    )
    gq_t = jnp.zeros((PAIR, 2 * P_SIZE), F32)
    for c in range(chunks):
        span = slice(c * P_SIZE, (c + 1) * P_SIZE)
        rows, keys, values, dkeys, dvalues = part(c)
        grad_prob = nt(values[rows, :], gcat)
        ds = (e_scr[span, :] * inverse * (grad_prob - row_dot)).astype(BF16)
        gq_t = gq_t + tn(keys[rows, :], ds)
        dkeys[rows, :] = nn(ds, qcat).astype(BF16)
        dvalues[rows, :] = nn(p_scr[span, :], gcat).astype(BF16)
    picked_q = jnp.concatenate([gq_t[:HD, :P_SIZE], gq_t[HD:, P_SIZE:]], axis=0)
    gq_ref[...] = (picked_q.T * (1.0 / math.sqrt(HD))).astype(BF16)


def return_kernel(sizes, rows_ref, wq, wkv, gin, attn, gq, dk, dv, base,
                  grad_out, wkv_out, wqo_out, base_out, rk, rv, *scratch):
    scatter_refs, (ss, rs) = scratch[:11], scratch[11:]
    place = Place(sizes)
    place.barrier()
    faces = place.faces()

    def face_copy(face, slot, which):
        source, target = ((dk, rk), (dv, rv))[which]
        return pltpu.make_async_remote_copy(
            src_ref=source.at[pl.ds((1 + face) * P_SIZE, P_SIZE)],
            dst_ref=target.at[slot],
            send_sem=ss.at[2 * face + which],
            recv_sem=rs.at[2 * slot + which],
            device_id=faces[face][1],
            device_id_type=MESH,
        )

    for face, (there, _) in enumerate(faces):
        @pl.when(there)
        def _(face=face):
            face_copy(face, face ^ 1, 0).start()
            face_copy(face, face ^ 1, 1).start()

        @pl.when(jnp.logical_not(there))
        def _(face=face):
            rk[face] = jnp.zeros((P_SIZE, D), BF16)
            rv[face] = jnp.zeros((P_SIZE, D), BF16)

    scatter = Scatter(place, base, scatter_refs)
    scatter.start(0)
    normed, inv_std = layer_norm(rows_ref[...].astype(F32))
    normed_low = normed.astype(BF16)
    wqo_out[:, :D] = tn(normed_low, gq[...]).astype(BF16)
    wqo_out[:, D:] = tn(attn[...], gin[...]).astype(BF16)
    scatter.finish(0)
    scatter.start(1)
    for face, (there, _) in enumerate(faces):
        @pl.when(there)
        def _(face=face):
            for which in range(2):
                face_copy(face, face ^ 1, which).wait_send()
                face_copy(face, face, which).wait_recv()
    scatter.finish(1)
    scatter.start(2)
    sum_k = dk[0:P_SIZE, :].astype(F32)
    sum_v = dv[0:P_SIZE, :].astype(F32)
    for face in range(6):
        sum_k = sum_k + rk[face].astype(F32)
        sum_v = sum_v + rv[face].astype(F32)
    pair_k = sum_k.astype(BF16)
    pair_v = sum_v.astype(BF16)
    wkv_out[:, :D] = tn(normed_low, pair_k).astype(BF16)
    wkv_out[:, D:] = tn(normed_low, pair_v).astype(BF16)
    scatter.finish(2)
    scatter.start(3)
    grad = nt(gq[...], wq[...]) + nt(pair_k, wkv[:, :D]) + nt(pair_v, wkv[:, D:])
    first_mean = jnp.mean(grad, axis=-1, keepdims=True)
    second_mean = jnp.mean(grad * normed, axis=-1, keepdims=True)
    grad_out[...] = (inv_std * (grad - first_mean - normed * second_mean)).astype(BF16)
    scatter.finish(3, base_out)


def scatter_kernel(sizes, source, out, *scratch):
    place = Place(sizes)
    place.barrier()
    scatter = Scatter(place, source, scratch)
    for level in range(4):
        scatter.start(level)
        scatter.finish(level, out if level == 3 else None)


def vmem():
    return pl.BlockSpec(memory_space=pltpu.VMEM)


def shape(dims, dtype):
    return jax.ShapeDtypeStruct(dims, dtype)


def remote(kernel, sizes, outs, scratch, collective, operands):
    return pl.pallas_call(
        functools.partial(kernel, sizes),
        out_shape=outs,
        in_specs=[vmem()] * len(operands),
        out_specs=jax.tree.map(lambda _: vmem(), outs),
        scratch_shapes=scratch,
        compiler_params=pltpu.CompilerParams(
            collective_id=collective, has_side_effects=True, vmem_limit_bytes=VMEM_BYTES
        ),
    )(*operands)


def attend(flags, q, g, keys, baffle):
    def cols(rows, shift):
        return pl.BlockSpec((rows, PAIR), lambda p: (0, p + shift))

    groups = D // PAIR
    return pl.pallas_call(
        attend_kernel,
        grid=(groups,),
        out_shape=(
            shape((P_SIZE, D), BF16),
            shape((P_SIZE, D), BF16),
            shape((NEAR, D), BF16),
            shape((NEAR, D), BF16),
            shape((NB, D), BF16),
            shape((NB, D), BF16),
        ),
        in_specs=[
            pl.BlockSpec(memory_space=pltpu.SMEM),
            cols(P_SIZE, 0),
            cols(P_SIZE, 0),
            cols(NEAR, 0),
            cols(NEAR, groups),
            pl.BlockSpec((NEAR, PAIR), lambda p: (0, 2 * groups)),
            cols(NB, 0),
            cols(NB, groups),
        ],
        out_specs=(
            cols(P_SIZE, 0),
            cols(P_SIZE, 0),
            cols(NEAR, 0),
            cols(NEAR, 0),
            cols(NB, 0),
            cols(NB, 0),
        ),
        scratch_shapes=[
            pltpu.VMEM((ALL, 2 * P_SIZE), F32),
            pltpu.VMEM((ALL, 2 * P_SIZE), BF16),
            pltpu.VMEM((8, LANES), BF16),
        ],
        compiler_params=pltpu.CompilerParams(vmem_limit_bytes=VMEM_BYTES),
    )(flags, q, g, keys, keys, keys, baffle, baffle)


def body(
    sizes,
    particles,
    log_weight,
    counts,
    pattern,
    query_weight,
    key_value_weight,
    output_weight,
    baffle_store,
    owner_device,
    cotangent,
):
    gx, gy, gz = sizes
    devices = gx * gy * gz
    rows_in = particles[0, 0, 0]
    valid_rows = jnp.arange(P_SIZE, dtype=jnp.int32) < counts[0, 0, 0]
    own_bias = jnp.where(valid_rows, log_weight[0, 0, 0], jnp.asarray(masked_bias, BF16))
    bias_lanes = jnp.broadcast_to(own_bias[:, None], (P_SIZE, LANES))
    grad_in = jnp.where(valid_rows[:, None], cotangent[0, 0, 0], jnp.zeros((), BF16))
    me = lax.axis_index(("gx", "gy", "gz"))
    width = NB * 2 * D // (devices * PIECE)
    pieces = (gx // 2, 2, gy, gz, PIECE, width)
    store = jnp.where(me == owner_device[0], baffle_store[0], jnp.zeros((), BF16)).reshape(pieces)
    copies = sum(n - 1 for _, _, n, _ in stage_plan(sizes)[1])
    dma = pltpu.SemaphoreType.DMA
    q, g, keys, final = remote(
        project_kernel,
        sizes,
        (
            shape((P_SIZE, D), BF16),
            shape((P_SIZE, D), BF16),
            shape((NEAR, AUG), BF16),
            shape(pieces, BF16),
        ),
        scatter_scratch(sizes, width)
        + [dma((copies,)), dma((copies,)), dma((6,)), dma((6,)), pltpu.VMEM((PIECE, width), BF16)],
        0,
        (rows_in, bias_lanes, query_weight, key_value_weight, output_weight, grad_in, store),
    )
    baffle = final.reshape(NB, 2 * D)
    attn, gq, dk, dv, dbk, dbv = attend(pattern[0, 0, 0], q, g, keys, baffle)
    projected = nn(attn, output_weight)
    update = jnp.where(valid_rows[:, None], projected, 0.0).astype(BF16)
    base = jnp.concatenate([dbk, dbv], axis=1).reshape(pieces)
    grad_rows, w_kv, w_qo, base_sum = remote(
        return_kernel,
        sizes,
        (
            shape((P_SIZE, D), BF16),
            shape((D, 2 * D), BF16),
            shape((D, 2 * D), BF16),
            shape((PIECE, width), F32),
        ),
        [pltpu.VMEM((6, P_SIZE, D), BF16), pltpu.VMEM((6, P_SIZE, D), BF16)]
        + scatter_scratch(sizes, width)
        + [dma((12,)), dma((12,))],
        1,
        (rows_in, query_weight, key_value_weight, grad_in, attn, gq, dk, dv, base),
    )
    if width == 2 * D:
        half = PIECE // 2
        weights = jnp.concatenate(
            [w_kv.reshape(devices, half, width), w_qo.reshape(devices, half, width)], axis=1
        )
    else:
        weights = jnp.concatenate(
            [
                w_kv.reshape(devices, -1),
                w_qo[:, :D].reshape(devices, -1),
                w_qo[:, D:].reshape(devices, -1),
            ],
            axis=1,
        )
    weight_sum = remote(
        scatter_kernel,
        sizes,
        shape((PIECE, width), F32),
        scatter_scratch(sizes, width),
        2,
        (weights.reshape(pieces),),
    )
    if width == 2 * D:
        grad_kv = weight_sum[:half].reshape(-1)
        grad_q = weight_sum[half:, :D].reshape(-1)
        grad_o = weight_sum[half:, D:].reshape(-1)
    else:
        flat = weight_sum.reshape(-1)
        part = D * D // devices
        grad_kv, grad_q, grad_o = flat[: 2 * part], flat[2 * part : 3 * part], flat[3 * part :]
    return (
        update[None, None, None],
        grad_rows[None, None, None],
        grad_q,
        grad_kv,
        grad_o,
        base_sum.reshape(-1),
    )


def solution(mesh):
    sizes = tuple(mesh.shape[axis] for axis in ("gx", "gy", "gz"))
    return jax.shard_map(
        functools.partial(body, sizes),
        mesh=mesh,
        in_specs=(
            P("gx", "gy", "gz", None, None),
            P("gx", "gy", "gz", None),
            P("gx", "gy", "gz"),
            P("gx", "gy", "gz", None),
            P(),
            P(),
            P(),
            P(("gx", "gy", "gz"), None, None),
            P(),
            P("gx", "gy", "gz", None, None),
        ),
        out_specs=(
            P("gx", "gy", "gz", None, None),
            P("gx", "gy", "gz", None, None),
            P(("gx", "gy", "gz")),
            P(("gx", "gy", "gz")),
            P(("gx", "gy", "gz")),
            P(("gx", "gy", "gz")),
        ),
        check_vma=False,
    )
```

```python
import functools
import math

import jax
import jax.numpy as jnp
from jax import lax
from jax.experimental import pallas as pl
from jax.experimental.pallas import tpu as pltpu
from jax.sharding import PartitionSpec as P

D = 512
H = 8
HD = 64
P_SIZE = 256
NB = 1024
LANES = 128
PAIR = 2 * HD
AUG = 2 * D + LANES
NEAR = 7 * P_SIZE
ALL = NEAR + NB
PIECE = 32

masked_bias = -1000000000.0
F32 = jnp.float32
BF16 = jnp.bfloat16
MESH = pl.DeviceIdType.MESH
VMEM_BYTES = 56 * 1024 * 1024


def nt(left, right):
    return lax.dot_general(left, right, (((1,), (1,)), ((), ())), preferred_element_type=F32)


def tn(left, right):
    return lax.dot_general(left, right, (((0,), (0,)), ((), ())), preferred_element_type=F32)


def nn(left, right):
    return jnp.dot(left, right, preferred_element_type=F32)


def layer_norm(values):
    row_mean = jnp.mean(values, axis=-1, keepdims=True)
    centered = values - row_mean
    inv_std = lax.rsqrt(jnp.mean(centered * centered, axis=-1, keepdims=True) + 1e-05)
    return (centered * inv_std, inv_std)


class Place:
    def __init__(self, sizes):
        self.sizes = sizes
        gx, gy, gz = sizes
        self.at = (lax.axis_index("gx"), lax.axis_index("gy"), lax.axis_index("gz"))
        self.counts = {"y": gx // 2, "c": 2, "gy": gy, "gz": gz}
        self.pos = {
            "y": self.at[0] // 2,
            "c": self.at[0] % 2,
            "gy": self.at[1],
            "gz": self.at[2],
        }

    def device(self, axis, position):
        pos = dict(self.pos)
        pos[axis] = position
        return (pos["y"] * 2 + pos["c"], pos["gy"], pos["gz"])

    def barrier(self):
        sem = pltpu.get_barrier_semaphore()
        total = 0
        for dim, count in enumerate(self.sizes):
            for step in range(1, count):
                target = list(self.at)
                target[dim] = lax.rem(self.at[dim] + step, count)
                pl.semaphore_signal(sem, inc=1, device_id=tuple(target), device_id_type=MESH)
                total += 1
        pl.semaphore_wait(sem, total)

    def faces(self):
        found = []
        for dim, count in enumerate(self.sizes):
            for side in (-1, 1):
                there = self.at[dim] > 0 if side < 0 else self.at[dim] < count - 1
                target = list(self.at)
                target[dim] = jnp.clip(self.at[dim] + side, 0, count - 1)
                found.append((there, tuple(target)))
        return found


AXES = ("y", "c", "gy", "gz")
ORDERS = (("c", "gz", "y", "gy"), ("c", "y", "gz", "gy"))


def select(fixed, rows):
    return tuple(fixed.get(axis, slice(None)) for axis in AXES) + (rows, slice(None))


def stage_plan(sizes):
    gx, gy, gz = sizes
    counts = {"y": gx // 2, "c": 2, "gy": gy, "gz": gz}
    plan = []
    for half, order in enumerate(ORDERS):
        done = []
        for axis in order:
            done.append(axis)
            left = tuple(counts[a] for a in AXES if a not in done)
            plan.append((half, axis, counts[axis], left))
    return counts, plan


def scatter_scratch(sizes, width):
    counts, plan = stage_plan(sizes)
    rows = PIECE // 2
    shapes = [pltpu.VMEM((n - 1,) + left + (rows, width), BF16) for _, _, n, left in plan]
    copies = sum(n - 1 for _, _, n, _ in plan)
    work = pltpu.VMEM((counts["y"], 2, counts["gy"], counts["gz"], PIECE, width), BF16)
    return shapes + [work, pltpu.SemaphoreType.DMA((copies,)), pltpu.SemaphoreType.DMA((copies,))]


class Scatter:
    def __init__(self, place, source, scratch):
        self.place = place
        self.source = source
        self.recv = scratch[:8]
        self.work, self.send_sem, self.recv_sem = scratch[8:11]
        self.plan = stage_plan(place.sizes)[1]
        self.offsets = []
        total = 0
        for _, _, n, _ in self.plan:
            self.offsets.append(total)
            total += n - 1

    def rows(self, half):
        return pl.ds(half * (PIECE // 2), PIECE // 2)

    def fixed(self, half, level):
        return {axis: self.place.pos[axis] for axis in ORDERS[half][:level]}

    def copies(self, half, level):
        at = half * 4 + level
        axis, n = self.plan[at][1], self.plan[at][2]
        origin = self.source if level == 0 else self.work
        found = []
        for step in range(1, n):
            target = lax.rem(self.place.pos[axis] + step, n)
            fixed = self.fixed(half, level)
            fixed[axis] = target
            found.append(
                pltpu.make_async_remote_copy(
                    src_ref=origin.at[select(fixed, self.rows(half))],
                    dst_ref=self.recv[at].at[step - 1],
                    send_sem=self.send_sem.at[self.offsets[at] + step - 1],
                    recv_sem=self.recv_sem.at[self.offsets[at] + step - 1],
                    device_id=self.place.device(axis, target),
                    device_id_type=MESH,
                )
            )
        return found

    def start(self, level, halves=(0, 1)):
        for half in halves:
            for copy in self.copies(half, level):
                copy.start()

    def finish(self, level, out=None, halves=(0, 1)):
        for half in halves:
            at = half * 4 + level
            for copy in self.copies(half, level):
                copy.wait()
            origin = self.source if level == 0 else self.work
            where = select(self.fixed(half, level + 1), self.rows(half))
            total = origin[where].astype(F32)
            for step in range(self.plan[at][2] - 1):
                total = total + self.recv[at][step].astype(F32)
            if out is None:
                self.work[where] = total.astype(BF16)
            else:
                out[self.rows(half), :] = total.astype(out.dtype)


def gather_copies(place, final, send_sem, recv_sem, level):
    counts, plan = stage_plan(place.sizes)
    found = []
    for half in range(2):
        order = ORDERS[half]
        axis = order[level]
        base = sum(n - 1 for h, a, n, _ in plan[: half * 4 + level])
        fixed = {a: place.pos[a] for a in order[: level + 1]}
        view = final.at[select(fixed, pl.ds(half * (PIECE // 2), PIECE // 2))]
        for step in range(1, counts[axis]):
            target = lax.rem(place.pos[axis] + step, counts[axis])
            found.append(
                pltpu.make_async_remote_copy(
                    src_ref=view,
                    dst_ref=view,
                    send_sem=send_sem.at[base + step - 1],
                    recv_sem=recv_sem.at[base + step - 1],
                    device_id=place.device(axis, target),
                    device_id_type=MESH,
                )
            )
    return found


def project_kernel(sizes, rows_ref, bias_ref, wq, wkv, wo, gin, baf, q_out, g_out, keys, final,
                   *scratch):
    scatter_refs, (gs, gr, hs, hr, piece) = scratch[:11], scratch[11:]
    place = Place(sizes)
    place.barrier()
    scatter = Scatter(place, baf, scatter_refs)
    scatter.start(0)
    normed_low = layer_norm(rows_ref[...].astype(F32))[0].astype(BF16)
    keys[0:P_SIZE, 0 : 2 * D] = nn(normed_low, wkv[...]).astype(BF16)
    keys[0:P_SIZE, 2 * D : AUG] = bias_ref[...]
    faces = place.faces()

    def face_copy(face, slot):
        return pltpu.make_async_remote_copy(
            src_ref=keys.at[pl.ds(0, P_SIZE)],
            dst_ref=keys.at[pl.ds((1 + slot) * P_SIZE, P_SIZE)],
            send_sem=hs.at[face],
            recv_sem=hr.at[slot],
            device_id=faces[face][1],
            device_id_type=MESH,
        )

    scatter.finish(0)
    scatter.start(1)
    def send_faces(wanted):
        for face in wanted:
            @pl.when(faces[face][0])
            def _(face=face):
                face_copy(face, face ^ 1).start()

            @pl.when(jnp.logical_not(faces[face][0]))
            def _(face=face):
                keys[(1 + face) * P_SIZE : (2 + face) * P_SIZE, :] = jnp.zeros((P_SIZE, AUG), BF16)

    send_faces((2, 3))
    q_out[...] = nn(normed_low, wq[...]).astype(BF16)
    g_out[...] = nt(gin[...], wo[...]).astype(BF16)
    scatter.finish(1)
    scatter.start(2)
    scatter.finish(2)
    scatter.start(3)
    send_faces((0, 1, 4, 5))
    scatter.finish(3, piece)
    final[place.pos["y"], place.pos["c"], place.pos["gy"], place.pos["gz"]] = piece[...]
    for level in (3, 2, 1, 0):
        sent = gather_copies(place, final, gs, gr, level)
        for copy in sent:
            copy.start()
        for copy in sent:
            copy.wait()
    for face, (there, _) in enumerate(faces):
        @pl.when(there)
        def _(face=face):
            face_copy(face, face ^ 1).wait_send()
            face_copy(face, face).wait_recv()


def attend_kernel(flags, q_ref, g_ref, k_ref, v_ref, b_ref, bk_ref, bv_ref,
                  attn_ref, gq_ref, dk_ref, dv_ref, dbk_ref, dbv_ref, e_scr, p_scr, d_scr):
    lane = lax.broadcasted_iota(jnp.int32, (P_SIZE, PAIR), 1)
    zero = jnp.zeros((P_SIZE, PAIR), BF16)
    q = q_ref[...] * jnp.asarray(1.0 / math.sqrt(HD), BF16)
    g = g_ref[...]
    qcat = jnp.concatenate([jnp.where(lane < HD, q, zero), jnp.where(lane < HD, zero, q)], axis=0)
    gcat = jnp.concatenate([jnp.where(lane < HD, g, zero), jnp.where(lane < HD, zero, g)], axis=0)
    first = (lax.broadcasted_iota(jnp.int32, (2 * P_SIZE, LANES), 1) == 0).astype(BF16)
    qaug = jnp.concatenate([qcat, first], axis=1)
    chunks = ALL // P_SIZE

    def part(c):
        if c < 7:
            return slice(c * P_SIZE, (c + 1) * P_SIZE), k_ref, v_ref, dk_ref, dv_ref
        return slice((c - 7) * P_SIZE, (c - 6) * P_SIZE), bk_ref, bv_ref, dbk_ref, dbv_ref

    top = jnp.full((8, 2 * P_SIZE), -3e38, F32)
    for c in range(chunks):
        rows, keys = part(c)[:2]
        if c < 7:
            bias = b_ref[rows, :]
            if c > 0:
                bias = jnp.where(flags[c - 1] == 1, bias, jnp.asarray(masked_bias, BF16))
            scores = nt(jnp.concatenate([keys[rows, :], bias], axis=1), qaug)
        else:
            scores = nt(keys[rows, :], qcat)
        e_scr[c * P_SIZE : (c + 1) * P_SIZE, :] = scores
        top = jnp.maximum(top, jnp.max(scores.reshape(P_SIZE // 8, 8, 2 * P_SIZE), axis=0))
    top = jnp.max(top, axis=0, keepdims=True)
    total = jnp.zeros((8, 2 * P_SIZE), F32)
    for c in range(chunks):
        span = slice(c * P_SIZE, (c + 1) * P_SIZE)
        e = jnp.exp(e_scr[span, :] - top)
        e_scr[span, :] = e
        total = total + jnp.sum(e.reshape(P_SIZE // 8, 8, 2 * P_SIZE), axis=0)
    inverse = 1.0 / jnp.sum(total, axis=0, keepdims=True)
    attn_t = jnp.zeros((PAIR, 2 * P_SIZE), F32)
    for c in range(chunks):
        span = slice(c * P_SIZE, (c + 1) * P_SIZE)
        rows, _, values = part(c)[:3]
        p = (e_scr[span, :] * inverse).astype(BF16)
        p_scr[span, :] = p
        attn_t = attn_t + tn(values[rows, :], p)
    picked = jnp.concatenate([attn_t[:HD, :P_SIZE], attn_t[HD:, P_SIZE:]], axis=0)
    attn_ref[...] = picked.T.astype(BF16)
    product = g.astype(F32).T * picked.astype(BF16).astype(F32)
    row_dot = jnp.concatenate(
        [
            jnp.sum(product[:HD], axis=0, keepdims=True),
            jnp.sum(product[HD:], axis=0, keepdims=True),
        ],
        axis=1,
    )
    gq_t = jnp.zeros((PAIR, 2 * P_SIZE), F32)
    for c in range(chunks):
        span = slice(c * P_SIZE, (c + 1) * P_SIZE)
        rows, keys, values, dkeys, dvalues = part(c)
        grad_prob = nt(values[rows, :], gcat)
        ds = (e_scr[span, :] * inverse * (grad_prob - row_dot)).astype(BF16)
        gq_t = gq_t + tn(keys[rows, :], ds)
        dkeys[rows, :] = nn(ds, qcat).astype(BF16)
        dvalues[rows, :] = nn(p_scr[span, :], gcat).astype(BF16)
    picked_q = jnp.concatenate([gq_t[:HD, :P_SIZE], gq_t[HD:, P_SIZE:]], axis=0)
    gq_ref[...] = (picked_q.T * (1.0 / math.sqrt(HD))).astype(BF16)


def return_kernel(sizes, rows_ref, wq, wkv, gin, attn, gq, dk, dv, base,
                  grad_out, wkv_out, wqo_out, base_out, rk, rv, *scratch):
    scatter_refs, (ss, rs) = scratch[:11], scratch[11:]
    place = Place(sizes)
    place.barrier()
    faces = place.faces()

    def face_copy(face, slot, which):
        source, target = ((dk, rk), (dv, rv))[which]
        return pltpu.make_async_remote_copy(
            src_ref=source.at[pl.ds((1 + face) * P_SIZE, P_SIZE)],
            dst_ref=target.at[slot],
            send_sem=ss.at[2 * face + which],
            recv_sem=rs.at[2 * slot + which],
            device_id=faces[face][1],
            device_id_type=MESH,
        )

    for face, (there, _) in enumerate(faces):
        @pl.when(there)
        def _(face=face):
            face_copy(face, face ^ 1, 0).start()
            face_copy(face, face ^ 1, 1).start()

        @pl.when(jnp.logical_not(there))
        def _(face=face):
            rk[face] = jnp.zeros((P_SIZE, D), BF16)
            rv[face] = jnp.zeros((P_SIZE, D), BF16)

    scatter = Scatter(place, base, scatter_refs)
    scatter.start(0)
    normed, inv_std = layer_norm(rows_ref[...].astype(F32))
    normed_low = normed.astype(BF16)
    wqo_out[:, :D] = tn(normed_low, gq[...]).astype(BF16)
    wqo_out[:, D:] = tn(attn[...], gin[...]).astype(BF16)
    scatter.finish(0)
    scatter.start(1)
    for face, (there, _) in enumerate(faces):
        @pl.when(there)
        def _(face=face):
            for which in range(2):
                face_copy(face, face ^ 1, which).wait_send()
                face_copy(face, face, which).wait_recv()
    scatter.finish(1)
    scatter.start(2)
    sum_k = dk[0:P_SIZE, :].astype(F32)
    sum_v = dv[0:P_SIZE, :].astype(F32)
    for face in range(6):
        sum_k = sum_k + rk[face].astype(F32)
        sum_v = sum_v + rv[face].astype(F32)
    pair_k = sum_k.astype(BF16)
    pair_v = sum_v.astype(BF16)
    wkv_out[:, :D] = tn(normed_low, pair_k).astype(BF16)
    wkv_out[:, D:] = tn(normed_low, pair_v).astype(BF16)
    scatter.finish(2)
    scatter.start(3)
    grad = nt(gq[...], wq[...]) + nt(pair_k, wkv[:, :D]) + nt(pair_v, wkv[:, D:])
    first_mean = jnp.mean(grad, axis=-1, keepdims=True)
    second_mean = jnp.mean(grad * normed, axis=-1, keepdims=True)
    grad_out[...] = (inv_std * (grad - first_mean - normed * second_mean)).astype(BF16)
    scatter.finish(3, base_out)


def scatter_kernel(sizes, source, out, *scratch):
    place = Place(sizes)
    place.barrier()
    scatter = Scatter(place, source, scratch)
    for level in range(4):
        scatter.start(level)
        scatter.finish(level, out if level == 3 else None)


def finish_kernel(sizes, count, rows_ref, wq, wkv, wo, gin, attn, gq, dk, dv, dbk, dbv,
                  update_out, grad_out, base_out, sum_out, rk, rv, base, weights, *scratch):
    base_refs, weight_refs, (ss, rs) = scratch[:11], scratch[11:22], scratch[22:]
    gx, gy, gz = sizes
    devices = gx * gy * gz
    half = PIECE // 2
    place = Place(sizes)
    place.barrier()
    faces = place.faces()

    def spread(target, rows, columns, values):
        step = values.shape[0] // devices
        for d in range(devices):
            x, y, z = d // (gy * gz), d // gz % gy, d % gz
            target[x // 2, x % 2, y, z, rows, columns] = values[d * step : (d + 1) * step]

    def face_copy(face, slot, which):
        source, target = ((dk, rk), (dv, rv))[which]
        return pltpu.make_async_remote_copy(
            src_ref=source.at[pl.ds((1 + face) * P_SIZE, P_SIZE)],
            dst_ref=target.at[slot],
            send_sem=ss.at[2 * face + which],
            recv_sem=rs.at[2 * slot + which],
            device_id=faces[face][1],
            device_id_type=MESH,
        )

    for face, (there, _) in enumerate(faces):
        @pl.when(there)
        def _(face=face):
            face_copy(face, face ^ 1, 0).start()
            face_copy(face, face ^ 1, 1).start()

        @pl.when(jnp.logical_not(there))
        def _(face=face):
            rk[face] = jnp.zeros((P_SIZE, D), BF16)
            rv[face] = jnp.zeros((P_SIZE, D), BF16)

    both, lower, upper = slice(0, PIECE), slice(0, half), slice(half, PIECE)
    left, right = slice(0, D), slice(D, 2 * D)
    spread(base, both, left, dbk[...])
    spread(base, both, right, dbv[...])
    first = Scatter(place, base, base_refs)
    second = Scatter(place, weights, weight_refs)
    first.start(0)
    normed, inv_std = layer_norm(rows_ref[...].astype(F32))
    normed_low = normed.astype(BF16)
    spread(weights, upper, left, tn(normed_low, gq[...]).astype(BF16))
    spread(weights, upper, right, tn(attn[...], gin[...]).astype(BF16))
    second.start(0, (1,))
    first.finish(0)
    first.start(1)
    slot = lax.broadcasted_iota(jnp.int32, (P_SIZE, D), 0)
    projected = nn(attn[...], wo[...])
    update_out[...] = jnp.where(slot < count[0], projected, 0.0).astype(BF16)
    second.finish(0, None, (1,))
    second.start(1, (1,))
    for face, (there, _) in enumerate(faces):
        @pl.when(there)
        def _(face=face):
            for which in range(2):
                face_copy(face, face ^ 1, which).wait_send()
                face_copy(face, face, which).wait_recv()
    sum_k = dk[0:P_SIZE, :].astype(F32)
    sum_v = dv[0:P_SIZE, :].astype(F32)
    for face in range(6):
        sum_k = sum_k + rk[face].astype(F32)
        sum_v = sum_v + rv[face].astype(F32)
    pair_k = sum_k.astype(BF16)
    pair_v = sum_v.astype(BF16)
    spread(weights, lower, left, tn(normed_low, pair_k).astype(BF16))
    spread(weights, lower, right, tn(normed_low, pair_v).astype(BF16))
    second.start(0, (0,))
    first.finish(1)
    first.start(2)
    second.finish(1, None, (1,))
    second.start(2, (1,))
    second.finish(0, None, (0,))
    second.start(1, (0,))
    grad = nt(gq[...], wq[...]) + nt(pair_k, wkv[:, :D]) + nt(pair_v, wkv[:, D:])
    first_mean = jnp.mean(grad, axis=-1, keepdims=True)
    second_mean = jnp.mean(grad * normed, axis=-1, keepdims=True)
    grad_out[...] = (inv_std * (grad - first_mean - normed * second_mean)).astype(BF16)
    first.finish(2)
    first.start(3)
    second.finish(2, None, (1,))
    second.start(3, (1,))
    second.finish(1, None, (0,))
    second.start(2, (0,))
    first.finish(3, base_out)
    second.finish(3, sum_out, (1,))
    second.finish(2, None, (0,))
    second.start(3, (0,))
    second.finish(3, sum_out, (0,))


def vmem():
    return pl.BlockSpec(memory_space=pltpu.VMEM)


def shape(dims, dtype):
    return jax.ShapeDtypeStruct(dims, dtype)


def remote(kernel, sizes, outs, scratch, collective, operands, scalars=0):
    return pl.pallas_call(
        functools.partial(kernel, sizes),
        out_shape=outs,
        in_specs=[pl.BlockSpec(memory_space=pltpu.SMEM)] * scalars
        + [vmem()] * (len(operands) - scalars),
        out_specs=jax.tree.map(lambda _: vmem(), outs),
        scratch_shapes=scratch,
        compiler_params=pltpu.CompilerParams(
            collective_id=collective, has_side_effects=True, vmem_limit_bytes=VMEM_BYTES
        ),
    )(*operands)


def attend(flags, q, g, keys, baffle):
    def cols(rows, shift):
        return pl.BlockSpec((rows, PAIR), lambda p: (0, p + shift))

    groups = D // PAIR
    return pl.pallas_call(
        attend_kernel,
        grid=(groups,),
        out_shape=(
            shape((P_SIZE, D), BF16),
            shape((P_SIZE, D), BF16),
            shape((NEAR, D), BF16),
            shape((NEAR, D), BF16),
            shape((NB, D), BF16),
            shape((NB, D), BF16),
        ),
        in_specs=[
            pl.BlockSpec(memory_space=pltpu.SMEM),
            cols(P_SIZE, 0),
            cols(P_SIZE, 0),
            cols(NEAR, 0),
            cols(NEAR, groups),
            pl.BlockSpec((NEAR, PAIR), lambda p: (0, 2 * groups)),
            cols(NB, 0),
            cols(NB, groups),
        ],
        out_specs=(
            cols(P_SIZE, 0),
            cols(P_SIZE, 0),
            cols(NEAR, 0),
            cols(NEAR, 0),
            cols(NB, 0),
            cols(NB, 0),
        ),
        scratch_shapes=[
            pltpu.VMEM((ALL, 2 * P_SIZE), F32),
            pltpu.VMEM((ALL, 2 * P_SIZE), BF16),
            pltpu.VMEM((8, LANES), BF16),
        ],
        compiler_params=pltpu.CompilerParams(vmem_limit_bytes=VMEM_BYTES),
    )(flags, q, g, keys, keys, keys, baffle, baffle)


def body(
    sizes,
    particles,
    log_weight,
    counts,
    pattern,
    query_weight,
    key_value_weight,
    output_weight,
    baffle_store,
    owner_device,
    cotangent,
):
    gx, gy, gz = sizes
    devices = gx * gy * gz
    rows_in = particles[0, 0, 0]
    valid_rows = jnp.arange(P_SIZE, dtype=jnp.int32) < counts[0, 0, 0]
    own_bias = jnp.where(valid_rows, log_weight[0, 0, 0], jnp.asarray(masked_bias, BF16))
    bias_lanes = jnp.broadcast_to(own_bias[:, None], (P_SIZE, LANES))
    grad_in = jnp.where(valid_rows[:, None], cotangent[0, 0, 0], jnp.zeros((), BF16))
    me = lax.axis_index(("gx", "gy", "gz"))
    width = NB * 2 * D // (devices * PIECE)
    pieces = (gx // 2, 2, gy, gz, PIECE, width)
    store = jnp.where(me == owner_device[0], baffle_store[0], jnp.zeros((), BF16)).reshape(pieces)
    copies = sum(n - 1 for _, _, n, _ in stage_plan(sizes)[1])
    dma = pltpu.SemaphoreType.DMA
    q, g, keys, final = remote(
        project_kernel,
        sizes,
        (
            shape((P_SIZE, D), BF16),
            shape((P_SIZE, D), BF16),
            shape((NEAR, AUG), BF16),
            shape(pieces, BF16),
        ),
        scatter_scratch(sizes, width)
        + [dma((copies,)), dma((copies,)), dma((6,)), dma((6,)), pltpu.VMEM((PIECE, width), BF16)],
        0,
        (rows_in, bias_lanes, query_weight, key_value_weight, output_weight, grad_in, store),
    )
    baffle = final.reshape(NB, 2 * D)
    attn, gq, dk, dv, dbk, dbv = attend(pattern[0, 0, 0], q, g, keys, baffle)
    halos = [pltpu.VMEM((6, P_SIZE, D), BF16), pltpu.VMEM((6, P_SIZE, D), BF16)]
    face_sems = [dma((12,)), dma((12,))]
    if width == 2 * D:
        half = PIECE // 2
        update, grad_rows, base_sum, weight_sum = remote(
            finish_kernel,
            sizes,
            (
                shape((P_SIZE, D), BF16),
                shape((P_SIZE, D), BF16),
                shape((PIECE, width), F32),
                shape((PIECE, width), F32),
            ),
            halos
            + [pltpu.VMEM(pieces, BF16), pltpu.VMEM(pieces, BF16)]
            + scatter_scratch(sizes, width)
            + scatter_scratch(sizes, width)
            + face_sems,
            1,
            (
                counts[0, 0],
                rows_in,
                query_weight,
                key_value_weight,
                output_weight,
                grad_in,
                attn,
                gq,
                dk,
                dv,
                dbk,
                dbv,
            ),
            1,
        )
        grad_kv = weight_sum[:half].reshape(-1)
        grad_q = weight_sum[half:, :D].reshape(-1)
        grad_o = weight_sum[half:, D:].reshape(-1)
    else:
        projected = nn(attn, output_weight)
        update = jnp.where(valid_rows[:, None], projected, 0.0).astype(BF16)
        base = jnp.concatenate([dbk, dbv], axis=1).reshape(pieces)
        grad_rows, w_kv, w_qo, base_sum = remote(
            return_kernel,
            sizes,
            (
                shape((P_SIZE, D), BF16),
                shape((D, 2 * D), BF16),
                shape((D, 2 * D), BF16),
                shape((PIECE, width), F32),
            ),
            halos + scatter_scratch(sizes, width) + face_sems,
            2,
            (rows_in, query_weight, key_value_weight, grad_in, attn, gq, dk, dv, base),
        )
        weights = jnp.concatenate(
            [
                w_kv.reshape(devices, -1),
                w_qo[:, :D].reshape(devices, -1),
                w_qo[:, D:].reshape(devices, -1),
            ],
            axis=1,
        )
        weight_sum = remote(
            scatter_kernel,
            sizes,
            shape((PIECE, width), F32),
            scatter_scratch(sizes, width),
            3,
            (weights.reshape(pieces),),
        )
        flat = weight_sum.reshape(-1)
        part = D * D // devices
        grad_kv, grad_q, grad_o = flat[: 2 * part], flat[2 * part : 3 * part], flat[3 * part :]
    return (
        update[None, None, None],
        grad_rows[None, None, None],
        grad_q,
        grad_kv,
        grad_o,
        base_sum.reshape(-1),
    )


def solution(mesh):
    sizes = tuple(mesh.shape[axis] for axis in ("gx", "gy", "gz"))
    return jax.shard_map(
        functools.partial(body, sizes),
        mesh=mesh,
        in_specs=(
            P("gx", "gy", "gz", None, None),
            P("gx", "gy", "gz", None),
            P("gx", "gy", "gz"),
            P("gx", "gy", "gz", None),
            P(),
            P(),
            P(),
            P(("gx", "gy", "gz"), None, None),
            P(),
            P("gx", "gy", "gz", None, None),
        ),
        out_specs=(
            P("gx", "gy", "gz", None, None),
            P("gx", "gy", "gz", None, None),
            P(("gx", "gy", "gz")),
            P(("gx", "gy", "gz")),
            P(("gx", "gy", "gz")),
            P(("gx", "gy", "gz")),
        ),
        check_vma=False,
    )
```

```python
import functools
import math

import jax
import jax.numpy as jnp
from jax import lax
from jax.experimental import pallas as pl
from jax.experimental.pallas import tpu as pltpu
from jax.sharding import PartitionSpec as P

D = 512
H = 8
HD = 64
P_SIZE = 256
NB = 1024
LANES = 128
PAIR = 2 * HD
AUG = 2 * D + LANES
NEAR = 7 * P_SIZE
ALL = NEAR + NB
PIECE = 32

masked_bias = -1000000000.0
F32 = jnp.float32
BF16 = jnp.bfloat16
MESH = pl.DeviceIdType.MESH
VMEM_BYTES = 56 * 1024 * 1024


def nt(left, right):
    return lax.dot_general(left, right, (((1,), (1,)), ((), ())), preferred_element_type=F32)


def tn(left, right):
    return lax.dot_general(left, right, (((0,), (0,)), ((), ())), preferred_element_type=F32)


def nn(left, right):
    return jnp.dot(left, right, preferred_element_type=F32)


def layer_norm(values):
    row_mean = jnp.mean(values, axis=-1, keepdims=True)
    centered = values - row_mean
    inv_std = lax.rsqrt(jnp.mean(centered * centered, axis=-1, keepdims=True) + 1e-05)
    return (centered * inv_std, inv_std)


class Place:
    def __init__(self, sizes):
        self.sizes = sizes
        gx, gy, gz = sizes
        self.at = (lax.axis_index("gx"), lax.axis_index("gy"), lax.axis_index("gz"))
        self.counts = {"y": gx // 2, "c": 2, "gy": gy, "gz": gz}
        self.pos = {
            "y": self.at[0] // 2,
            "c": self.at[0] % 2,
            "gy": self.at[1],
            "gz": self.at[2],
        }

    def device(self, axis, position):
        pos = dict(self.pos)
        pos[axis] = position
        return (pos["y"] * 2 + pos["c"], pos["gy"], pos["gz"])

    def barrier(self):
        sem = pltpu.get_barrier_semaphore()
        total = 0
        for dim, count in enumerate(self.sizes):
            for step in range(1, count):
                target = list(self.at)
                target[dim] = lax.rem(self.at[dim] + step, count)
                pl.semaphore_signal(sem, inc=1, device_id=tuple(target), device_id_type=MESH)
                total += 1
        pl.semaphore_wait(sem, total)

    def faces(self):
        found = []
        for dim, count in enumerate(self.sizes):
            for side in (-1, 1):
                there = self.at[dim] > 0 if side < 0 else self.at[dim] < count - 1
                target = list(self.at)
                target[dim] = jnp.clip(self.at[dim] + side, 0, count - 1)
                found.append((there, tuple(target)))
        return found


AXES = ("y", "c", "gy", "gz")
ORDERS = (("c", "gz", "y", "gy"), ("c", "y", "gz", "gy"))


def select(fixed, rows, columns=slice(None)):
    return tuple(fixed.get(axis, slice(None)) for axis in AXES) + (rows, columns)


def stage_plan(sizes):
    gx, gy, gz = sizes
    counts = {"y": gx // 2, "c": 2, "gy": gy, "gz": gz}
    plan = []
    for half, order in enumerate(ORDERS):
        done = []
        for axis in order:
            done.append(axis)
            left = tuple(counts[a] for a in AXES if a not in done)
            plan.append((half, axis, counts[axis], left))
    return counts, plan


def scatter_scratch(sizes, width):
    counts, plan = stage_plan(sizes)
    rows = PIECE // 2
    shapes = [pltpu.VMEM((n - 1,) + left + (rows, width), BF16) for _, _, n, left in plan]
    copies = sum(n - 1 for _, _, n, _ in plan)
    work = pltpu.VMEM((counts["y"], 2, counts["gy"], counts["gz"], PIECE, width), BF16)
    return shapes + [work, pltpu.SemaphoreType.DMA((copies,)), pltpu.SemaphoreType.DMA((copies,))]


class Scatter:
    def __init__(self, place, source, scratch, columns=slice(None)):
        self.place = place
        self.columns = columns
        self.source = source
        self.recv = scratch[:8]
        self.work, self.send_sem, self.recv_sem = scratch[8:11]
        self.plan = stage_plan(place.sizes)[1]
        self.offsets = []
        total = 0
        for _, _, n, _ in self.plan:
            self.offsets.append(total)
            total += n - 1

    def rows(self, half):
        return pl.ds(half * (PIECE // 2), PIECE // 2)

    def fixed(self, half, level):
        return {axis: self.place.pos[axis] for axis in ORDERS[half][:level]}

    def copies(self, half, level):
        at = half * 4 + level
        axis, n = self.plan[at][1], self.plan[at][2]
        origin = self.source if level == 0 else self.work
        columns = self.columns if level == 0 else slice(None)
        found = []
        for step in range(1, n):
            target = lax.rem(self.place.pos[axis] + step, n)
            fixed = self.fixed(half, level)
            fixed[axis] = target
            found.append(
                pltpu.make_async_remote_copy(
                    src_ref=origin.at[select(fixed, self.rows(half), columns)],
                    dst_ref=self.recv[at].at[step - 1],
                    send_sem=self.send_sem.at[self.offsets[at] + step - 1],
                    recv_sem=self.recv_sem.at[self.offsets[at] + step - 1],
                    device_id=self.place.device(axis, target),
                    device_id_type=MESH,
                )
            )
        return found

    def start(self, level, halves=(0, 1)):
        for half in halves:
            for copy in self.copies(half, level):
                copy.start()

    def finish(self, level, out=None, halves=(0, 1)):
        for half in halves:
            at = half * 4 + level
            for copy in self.copies(half, level):
                copy.wait()
            origin = self.source if level == 0 else self.work
            where = select(self.fixed(half, level + 1), self.rows(half))
            taken = where[:-1] + ((self.columns if level == 0 else slice(None)),)
            total = origin[taken].astype(F32)
            for step in range(self.plan[at][2] - 1):
                total = total + self.recv[at][step].astype(F32)
            if out is None:
                self.work[where] = total.astype(BF16)
            else:
                out[self.rows(half), self.columns] = total.astype(out.dtype)

    def advance(self, level, halves=(0, 1)):
        for half in halves:
            self.finish(level, None, (half,))
            self.start(level + 1, (half,))


def gather_copies(place, final, send_sem, recv_sem, level, group, half, columns):
    counts, plan = stage_plan(place.sizes)
    order = ORDERS[half]
    axis = order[level]
    base = sum(n - 1 for _, _, n, _ in plan[: half * 4 + level])
    base += group * sum(n - 1 for _, _, n, _ in plan)
    fixed = {a: place.pos[a] for a in order[: level + 1]}
    view = final.at[select(fixed, pl.ds(half * (PIECE // 2), PIECE // 2), columns)]
    found = []
    for step in range(1, counts[axis]):
        target = lax.rem(place.pos[axis] + step, counts[axis])
        found.append(
            pltpu.make_async_remote_copy(
                src_ref=view,
                dst_ref=view,
                send_sem=send_sem.at[base + step - 1],
                recv_sem=recv_sem.at[base + step - 1],
                device_id=place.device(axis, target),
                device_id_type=MESH,
            )
        )
    return found


def groups_of(width):
    return 2 if width % (2 * LANES) == 0 else 1


def project_kernel(sizes, rows_ref, bias_ref, wq, wkv, wo, gin, baf, q_out, g_out, keys, final,
                   *scratch):
    width = baf.shape[-1]
    groups = groups_of(width)
    gs, gr, hs, hr = scratch[11 * groups :]
    place = Place(sizes)
    place.barrier()
    columns = [slice(g * (width // groups), (g + 1) * (width // groups)) for g in range(groups)]
    scatters = [
        Scatter(place, baf, scratch[11 * g : 11 * g + 11], columns[g]) for g in range(groups)
    ]
    for scatter in scatters:
        scatter.start(0)
    normed_low = layer_norm(rows_ref[...].astype(F32))[0].astype(BF16)
    keys[0:P_SIZE, 0 : 2 * D] = nn(normed_low, wkv[...]).astype(BF16)
    keys[0:P_SIZE, 2 * D : AUG] = bias_ref[...]
    faces = place.faces()

    def face_copy(face, slot):
        return pltpu.make_async_remote_copy(
            src_ref=keys.at[pl.ds(0, P_SIZE)],
            dst_ref=keys.at[pl.ds((1 + slot) * P_SIZE, P_SIZE)],
            send_sem=hs.at[face],
            recv_sem=hr.at[slot],
            device_id=faces[face][1],
            device_id_type=MESH,
        )

    for scatter in scatters:
        scatter.advance(0)

    def send_faces(wanted):
        for face in wanted:
            @pl.when(faces[face][0])
            def _(face=face):
                face_copy(face, face ^ 1).start()

            @pl.when(jnp.logical_not(faces[face][0]))
            def _(face=face):
                keys[(1 + face) * P_SIZE : (2 + face) * P_SIZE, :] = jnp.zeros((P_SIZE, AUG), BF16)

    send_faces((2, 3))
    q_out[...] = nn(normed_low, wq[...]).astype(BF16)
    g_out[...] = nt(gin[...], wo[...]).astype(BF16)
    for level in (1, 2):
        for scatter in scatters:
            scatter.advance(level)
    send_faces((0, 1, 4, 5))
    mine = final.at[place.pos["y"], place.pos["c"], place.pos["gy"], place.pos["gz"]]
    streams = [(g, half) for g in range(groups) for half in range(2)]

    def spread_copies(level, g, half):
        return gather_copies(place, final, gs, gr, level, g, half, columns[g])

    for g, half in streams:
        scatters[g].finish(3, mine, (half,))
        for copy in spread_copies(3, g, half):
            copy.start()
    for level in (3, 2, 1, 0):
        for g, half in streams:
            for copy in spread_copies(level, g, half):
                copy.wait()
            if level > 0:
                for copy in spread_copies(level - 1, g, half):
                    copy.start()
    for face, (there, _) in enumerate(faces):
        @pl.when(there)
        def _(face=face):
            face_copy(face, face ^ 1).wait_send()
            face_copy(face, face).wait_recv()


def attend_kernel(flags, count, q_ref, g_ref, k_ref, v_ref, b_ref, bk_ref, bv_ref, wo_ref,
                  update_ref, attn_ref, gq_ref, dk_ref, dv_ref, dbk_ref, dbv_ref, e_scr, p_scr, u_scr):
    lane = lax.broadcasted_iota(jnp.int32, (P_SIZE, PAIR), 1)
    zero = jnp.zeros((P_SIZE, PAIR), BF16)
    q = q_ref[...] * jnp.asarray(1.0 / math.sqrt(HD), BF16)
    g = g_ref[...]
    qcat = jnp.concatenate([jnp.where(lane < HD, q, zero), jnp.where(lane < HD, zero, q)], axis=0)
    gcat = jnp.concatenate([jnp.where(lane < HD, g, zero), jnp.where(lane < HD, zero, g)], axis=0)
    first = (lax.broadcasted_iota(jnp.int32, (2 * P_SIZE, LANES), 1) == 0).astype(BF16)
    qaug = jnp.concatenate([qcat, first], axis=1)
    chunks = ALL // P_SIZE

    def part(c):
        if c < 7:
            return slice(c * P_SIZE, (c + 1) * P_SIZE), k_ref, v_ref, dk_ref, dv_ref
        return slice((c - 7) * P_SIZE, (c - 6) * P_SIZE), bk_ref, bv_ref, dbk_ref, dbv_ref

    top = jnp.full((8, 2 * P_SIZE), -3e38, F32)
    for c in range(chunks):
        rows, keys = part(c)[:2]
        if c < 7:
            bias = b_ref[rows, :]
            if c > 0:
                bias = jnp.where(flags[c - 1] == 1, bias, jnp.asarray(masked_bias, BF16))
            scores = nt(jnp.concatenate([keys[rows, :], bias], axis=1), qaug)
        else:
            scores = nt(keys[rows, :], qcat)
        e_scr[c * P_SIZE : (c + 1) * P_SIZE, :] = scores
        top = jnp.maximum(top, jnp.max(scores.reshape(P_SIZE // 8, 8, 2 * P_SIZE), axis=0))
    top = jnp.max(top, axis=0, keepdims=True)
    total = jnp.zeros((8, 2 * P_SIZE), F32)
    for c in range(chunks):
        span = slice(c * P_SIZE, (c + 1) * P_SIZE)
        e = jnp.exp(e_scr[span, :] - top)
        e_scr[span, :] = e
        total = total + jnp.sum(e.reshape(P_SIZE // 8, 8, 2 * P_SIZE), axis=0)
    inverse = 1.0 / jnp.sum(total, axis=0, keepdims=True)
    attn_t = jnp.zeros((PAIR, 2 * P_SIZE), F32)
    for c in range(chunks):
        span = slice(c * P_SIZE, (c + 1) * P_SIZE)
        rows, _, values = part(c)[:3]
        p = (e_scr[span, :] * inverse).astype(BF16)
        p_scr[span, :] = p
        attn_t = attn_t + tn(values[rows, :], p)
    picked = jnp.concatenate([attn_t[:HD, :P_SIZE], attn_t[HD:, P_SIZE:]], axis=0)
    attn = picked.T.astype(BF16)
    attn_ref[...] = attn
    step = pl.program_id(0)
    projected = nn(attn, wo_ref[...])

    @pl.when(step == 0)
    def _():
        u_scr[...] = projected

    @pl.when(step > 0)
    def _():
        u_scr[...] += projected

    @pl.when(step == D // PAIR - 1)
    def _():
        slot = lax.broadcasted_iota(jnp.int32, (P_SIZE, D), 0)
        update_ref[...] = jnp.where(slot < count[0], u_scr[...], 0.0).astype(BF16)

    product = g.astype(F32).T * picked.astype(BF16).astype(F32)
    row_dot = jnp.concatenate(
        [
            jnp.sum(product[:HD], axis=0, keepdims=True),
            jnp.sum(product[HD:], axis=0, keepdims=True),
        ],
        axis=1,
    )
    gq_t = jnp.zeros((PAIR, 2 * P_SIZE), F32)
    for c in range(chunks):
        span = slice(c * P_SIZE, (c + 1) * P_SIZE)
        rows, keys, values, dkeys, dvalues = part(c)
        grad_prob = nt(values[rows, :], gcat)
        ds = (e_scr[span, :] * inverse * (grad_prob - row_dot)).astype(BF16)
        gq_t = gq_t + tn(keys[rows, :], ds)
        dkeys[rows, :] = nn(ds, qcat).astype(BF16)
        dvalues[rows, :] = nn(p_scr[span, :], gcat).astype(BF16)
    picked_q = jnp.concatenate([gq_t[:HD, :P_SIZE], gq_t[HD:, P_SIZE:]], axis=0)
    gq_ref[...] = (picked_q.T * (1.0 / math.sqrt(HD))).astype(BF16)


def return_kernel(sizes, rows_ref, wq, wkv, gin, attn, gq, dk, dv, base,
                  grad_out, wkv_out, wqo_out, base_out, rk, rv, *scratch):
    scatter_refs, (ss, rs) = scratch[:11], scratch[11:]
    place = Place(sizes)
    place.barrier()
    faces = place.faces()

    def face_copy(face, slot, which):
        source, target = ((dk, rk), (dv, rv))[which]
        return pltpu.make_async_remote_copy(
            src_ref=source.at[pl.ds((1 + face) * P_SIZE, P_SIZE)],
            dst_ref=target.at[slot],
            send_sem=ss.at[2 * face + which],
            recv_sem=rs.at[2 * slot + which],
            device_id=faces[face][1],
            device_id_type=MESH,
        )

    for face, (there, _) in enumerate(faces):
        @pl.when(there)
        def _(face=face):
            face_copy(face, face ^ 1, 0).start()
            face_copy(face, face ^ 1, 1).start()

        @pl.when(jnp.logical_not(there))
        def _(face=face):
            rk[face] = jnp.zeros((P_SIZE, D), BF16)
            rv[face] = jnp.zeros((P_SIZE, D), BF16)

    scatter = Scatter(place, base, scatter_refs)
    scatter.start(0)
    normed, inv_std = layer_norm(rows_ref[...].astype(F32))
    normed_low = normed.astype(BF16)
    wqo_out[:, :D] = tn(normed_low, gq[...]).astype(BF16)
    wqo_out[:, D:] = tn(attn[...], gin[...]).astype(BF16)
    scatter.finish(0)
    scatter.start(1)
    for face, (there, _) in enumerate(faces):
        @pl.when(there)
        def _(face=face):
            for which in range(2):
                face_copy(face, face ^ 1, which).wait_send()
                face_copy(face, face, which).wait_recv()
    scatter.finish(1)
    scatter.start(2)
    sum_k = dk[0:P_SIZE, :].astype(F32)
    sum_v = dv[0:P_SIZE, :].astype(F32)
    for face in range(6):
        sum_k = sum_k + rk[face].astype(F32)
        sum_v = sum_v + rv[face].astype(F32)
    pair_k = sum_k.astype(BF16)
    pair_v = sum_v.astype(BF16)
    wkv_out[:, :D] = tn(normed_low, pair_k).astype(BF16)
    wkv_out[:, D:] = tn(normed_low, pair_v).astype(BF16)
    scatter.finish(2)
    scatter.start(3)
    grad = nt(gq[...], wq[...]) + nt(pair_k, wkv[:, :D]) + nt(pair_v, wkv[:, D:])
    first_mean = jnp.mean(grad, axis=-1, keepdims=True)
    second_mean = jnp.mean(grad * normed, axis=-1, keepdims=True)
    grad_out[...] = (inv_std * (grad - first_mean - normed * second_mean)).astype(BF16)
    scatter.finish(3, base_out)


def scatter_kernel(sizes, source, out, *scratch):
    place = Place(sizes)
    place.barrier()
    scatter = Scatter(place, source, scratch)
    for level in range(4):
        scatter.start(level)
        scatter.finish(level, out if level == 3 else None)


def finish_kernel(sizes, rows_ref, wq, wkv, gin, attn, gq, dk, dv, dbk, dbv,
                  grad_out, base_out, sum_out, rk, rv, base, weights, *scratch):
    base_refs, weight_refs, (ss, rs) = scratch[:11], scratch[11:22], scratch[22:]
    gx, gy, gz = sizes
    devices = gx * gy * gz
    half = PIECE // 2
    place = Place(sizes)
    place.barrier()
    faces = place.faces()

    def spread(target, rows, columns, values):
        step = values.shape[0] // devices
        for d in range(devices):
            x, y, z = d // (gy * gz), d // gz % gy, d % gz
            target[x // 2, x % 2, y, z, rows, columns] = values[d * step : (d + 1) * step]

    def face_copy(face, slot, which):
        source, target = ((dk, rk), (dv, rv))[which]
        return pltpu.make_async_remote_copy(
            src_ref=source.at[pl.ds((1 + face) * P_SIZE, P_SIZE)],
            dst_ref=target.at[slot],
            send_sem=ss.at[2 * face + which],
            recv_sem=rs.at[2 * slot + which],
            device_id=faces[face][1],
            device_id_type=MESH,
        )

    for face, (there, _) in enumerate(faces):
        @pl.when(there)
        def _(face=face):
            face_copy(face, face ^ 1, 0).start()
            face_copy(face, face ^ 1, 1).start()

        @pl.when(jnp.logical_not(there))
        def _(face=face):
            rk[face] = jnp.zeros((P_SIZE, D), BF16)
            rv[face] = jnp.zeros((P_SIZE, D), BF16)

    both, lower, upper = slice(0, PIECE), slice(0, half), slice(half, PIECE)
    left, right = slice(0, D), slice(D, 2 * D)
    spread(base, both, left, dbk[...])
    spread(base, both, right, dbv[...])
    first = Scatter(place, base, base_refs)
    second = Scatter(place, weights, weight_refs)
    first.start(0)
    normed, inv_std = layer_norm(rows_ref[...].astype(F32))
    normed_low = normed.astype(BF16)
    spread(weights, upper, left, tn(normed_low, gq[...]).astype(BF16))
    spread(weights, upper, right, tn(attn[...], gin[...]).astype(BF16))
    second.start(0, (1,))
    first.advance(0)
    second.advance(0, (1,))
    for face, (there, _) in enumerate(faces):
        @pl.when(there)
        def _(face=face):
            for which in range(2):
                face_copy(face, face ^ 1, which).wait_send()
                face_copy(face, face, which).wait_recv()
    sum_k = dk[0:P_SIZE, :].astype(F32)
    sum_v = dv[0:P_SIZE, :].astype(F32)
    for face in range(6):
        sum_k = sum_k + rk[face].astype(F32)
        sum_v = sum_v + rv[face].astype(F32)
    pair_k = sum_k.astype(BF16)
    pair_v = sum_v.astype(BF16)
    spread(weights, lower, left, tn(normed_low, pair_k).astype(BF16))
    spread(weights, lower, right, tn(normed_low, pair_v).astype(BF16))
    second.start(0, (0,))
    first.advance(1)
    second.advance(1, (1,))
    second.advance(0, (0,))
    grad = nt(gq[...], wq[...]) + nt(pair_k, wkv[:, :D]) + nt(pair_v, wkv[:, D:])
    first_mean = jnp.mean(grad, axis=-1, keepdims=True)
    second_mean = jnp.mean(grad * normed, axis=-1, keepdims=True)
    grad_out[...] = (inv_std * (grad - first_mean - normed * second_mean)).astype(BF16)
    first.advance(2)
    second.advance(2, (1,))
    second.advance(1, (0,))
    first.finish(3, base_out)
    second.finish(3, sum_out, (1,))
    second.advance(2, (0,))
    second.finish(3, sum_out, (0,))


def vmem():
    return pl.BlockSpec(memory_space=pltpu.VMEM)


def shape(dims, dtype):
    return jax.ShapeDtypeStruct(dims, dtype)


def remote(kernel, sizes, outs, scratch, collective, operands):
    return pl.pallas_call(
        functools.partial(kernel, sizes),
        out_shape=outs,
        in_specs=[vmem()] * len(operands),
        out_specs=jax.tree.map(lambda _: vmem(), outs),
        scratch_shapes=scratch,
        compiler_params=pltpu.CompilerParams(
            collective_id=collective, has_side_effects=True, vmem_limit_bytes=VMEM_BYTES
        ),
    )(*operands)


def attend(flags, count, q, g, keys, baffle, output_weight):
    def cols(rows, shift):
        return pl.BlockSpec((rows, PAIR), lambda p: (0, p + shift))

    groups = D // PAIR
    return pl.pallas_call(
        attend_kernel,
        grid=(groups,),
        out_shape=(
            shape((P_SIZE, D), BF16),
            shape((P_SIZE, D), BF16),
            shape((P_SIZE, D), BF16),
            shape((NEAR, D), BF16),
            shape((NEAR, D), BF16),
            shape((NB, D), BF16),
            shape((NB, D), BF16),
        ),
        in_specs=[
            pl.BlockSpec(memory_space=pltpu.SMEM),
            pl.BlockSpec(memory_space=pltpu.SMEM),
            cols(P_SIZE, 0),
            cols(P_SIZE, 0),
            cols(NEAR, 0),
            cols(NEAR, groups),
            pl.BlockSpec((NEAR, PAIR), lambda p: (0, 2 * groups)),
            cols(NB, 0),
            cols(NB, groups),
            pl.BlockSpec((PAIR, D), lambda p: (p, 0)),
        ],
        out_specs=(
            pl.BlockSpec((P_SIZE, D), lambda p: (0, 0)),
            cols(P_SIZE, 0),
            cols(P_SIZE, 0),
            cols(NEAR, 0),
            cols(NEAR, 0),
            cols(NB, 0),
            cols(NB, 0),
        ),
        scratch_shapes=[
            pltpu.VMEM((ALL, 2 * P_SIZE), F32),
            pltpu.VMEM((ALL, 2 * P_SIZE), BF16),
            pltpu.VMEM((P_SIZE, D), F32),
        ],
        compiler_params=pltpu.CompilerParams(vmem_limit_bytes=VMEM_BYTES),
    )(flags, count, q, g, keys, keys, keys, baffle, baffle, output_weight)


def body(
    sizes,
    particles,
    log_weight,
    counts,
    pattern,
    query_weight,
    key_value_weight,
    output_weight,
    baffle_store,
    owner_device,
    cotangent,
):
    gx, gy, gz = sizes
    devices = gx * gy * gz
    rows_in = particles[0, 0, 0]
    valid_rows = jnp.arange(P_SIZE, dtype=jnp.int32) < counts[0, 0, 0]
    own_bias = jnp.where(valid_rows, log_weight[0, 0, 0], jnp.asarray(masked_bias, BF16))
    bias_lanes = jnp.broadcast_to(own_bias[:, None], (P_SIZE, LANES))
    grad_in = jnp.where(valid_rows[:, None], cotangent[0, 0, 0], jnp.zeros((), BF16))
    me = lax.axis_index(("gx", "gy", "gz"))
    width = NB * 2 * D // (devices * PIECE)
    pieces = (gx // 2, 2, gy, gz, PIECE, width)
    store = jnp.where(me == owner_device[0], baffle_store[0], jnp.zeros((), BF16)).reshape(pieces)
    groups = groups_of(width)
    copies = groups * sum(n - 1 for _, _, n, _ in stage_plan(sizes)[1])
    dma = pltpu.SemaphoreType.DMA
    q, g, keys, final = remote(
        project_kernel,
        sizes,
        (
            shape((P_SIZE, D), BF16),
            shape((P_SIZE, D), BF16),
            shape((NEAR, AUG), BF16),
            shape(pieces, BF16),
        ),
        scatter_scratch(sizes, width // groups) * groups
        + [dma((copies,)), dma((copies,)), dma((6,)), dma((6,))],
        0,
        (rows_in, bias_lanes, query_weight, key_value_weight, output_weight, grad_in, store),
    )
    baffle = final.reshape(NB, 2 * D)
    update, attn, gq, dk, dv, dbk, dbv = attend(
        pattern[0, 0, 0], counts[0, 0], q, g, keys, baffle, output_weight
    )
    halos = [pltpu.VMEM((6, P_SIZE, D), BF16), pltpu.VMEM((6, P_SIZE, D), BF16)]
    face_sems = [dma((12,)), dma((12,))]
    if width == 2 * D:
        half = PIECE // 2
        grad_rows, base_sum, weight_sum = remote(
            finish_kernel,
            sizes,
            (
                shape((P_SIZE, D), BF16),
                shape((PIECE, width), F32),
                shape((PIECE, width), F32),
            ),
            halos
            + [pltpu.VMEM(pieces, BF16), pltpu.VMEM(pieces, BF16)]
            + scatter_scratch(sizes, width)
            + scatter_scratch(sizes, width)
            + face_sems,
            1,
            (
                rows_in,
                query_weight,
                key_value_weight,
                grad_in,
                attn,
                gq,
                dk,
                dv,
                dbk,
                dbv,
            ),
        )
        grad_kv = weight_sum[:half].reshape(-1)
        grad_q = weight_sum[half:, :D].reshape(-1)
        grad_o = weight_sum[half:, D:].reshape(-1)
    else:
        base = jnp.concatenate([dbk, dbv], axis=1).reshape(pieces)
        grad_rows, w_kv, w_qo, base_sum = remote(
            return_kernel,
            sizes,
            (
                shape((P_SIZE, D), BF16),
                shape((D, 2 * D), BF16),
                shape((D, 2 * D), BF16),
                shape((PIECE, width), F32),
            ),
            halos + scatter_scratch(sizes, width) + face_sems,
            2,
            (rows_in, query_weight, key_value_weight, grad_in, attn, gq, dk, dv, base),
        )
        weights = jnp.concatenate(
            [
                w_kv.reshape(devices, -1),
                w_qo[:, :D].reshape(devices, -1),
                w_qo[:, D:].reshape(devices, -1),
            ],
            axis=1,
        )
        weight_sum = remote(
            scatter_kernel,
            sizes,
            shape((PIECE, width), F32),
            scatter_scratch(sizes, width),
            3,
            (weights.reshape(pieces),),
        )
        flat = weight_sum.reshape(-1)
        part = D * D // devices
        grad_kv, grad_q, grad_o = flat[: 2 * part], flat[2 * part : 3 * part], flat[3 * part :]
    return (
        update[None, None, None],
        grad_rows[None, None, None],
        grad_q,
        grad_kv,
        grad_o,
        base_sum.reshape(-1),
    )


def solution(mesh):
    sizes = tuple(mesh.shape[axis] for axis in ("gx", "gy", "gz"))
    return jax.shard_map(
        functools.partial(body, sizes),
        mesh=mesh,
        in_specs=(
            P("gx", "gy", "gz", None, None),
            P("gx", "gy", "gz", None),
            P("gx", "gy", "gz"),
            P("gx", "gy", "gz", None),
            P(),
            P(),
            P(),
            P(("gx", "gy", "gz"), None, None),
            P(),
            P("gx", "gy", "gz", None, None),
        ),
        out_specs=(
            P("gx", "gy", "gz", None, None),
            P("gx", "gy", "gz", None, None),
            P(("gx", "gy", "gz")),
            P(("gx", "gy", "gz")),
            P(("gx", "gy", "gz")),
            P(("gx", "gy", "gz")),
        ),
        check_vma=False,
    )
```

```python
import functools
import math

import jax
import jax.numpy as jnp
from jax import lax
from jax.experimental import pallas as pl
from jax.experimental.pallas import tpu as pltpu
from jax.sharding import PartitionSpec as P

D = 512
H = 8
HD = 64
P_SIZE = 256
NB = 1024
LANES = 128
PAIR = 2 * HD
AUG = 2 * D + LANES
NEAR = 7 * P_SIZE
ALL = NEAR + NB
PIECE = 32

masked_bias = -1000000000.0
F32 = jnp.float32
BF16 = jnp.bfloat16
MESH = pl.DeviceIdType.MESH
VMEM_BYTES = 56 * 1024 * 1024


def nt(left, right):
    return lax.dot_general(left, right, (((1,), (1,)), ((), ())), preferred_element_type=F32)


def tn(left, right):
    return lax.dot_general(left, right, (((0,), (0,)), ((), ())), preferred_element_type=F32)


def nn(left, right):
    return jnp.dot(left, right, preferred_element_type=F32)


def layer_norm(values):
    row_mean = jnp.mean(values, axis=-1, keepdims=True)
    centered = values - row_mean
    inv_std = lax.rsqrt(jnp.mean(centered * centered, axis=-1, keepdims=True) + 1e-05)
    return (centered * inv_std, inv_std)


class Place:
    def __init__(self, sizes):
        self.sizes = sizes
        gx, gy, gz = sizes
        self.at = (lax.axis_index("gx"), lax.axis_index("gy"), lax.axis_index("gz"))
        self.counts = {"y": gx // 2, "c": 2, "gy": gy, "gz": gz}
        self.pos = {
            "y": self.at[0] // 2,
            "c": self.at[0] % 2,
            "gy": self.at[1],
            "gz": self.at[2],
        }

    def device(self, axis, position):
        pos = dict(self.pos)
        pos[axis] = position
        return (pos["y"] * 2 + pos["c"], pos["gy"], pos["gz"])

    def barrier(self):
        sem = pltpu.get_barrier_semaphore()
        total = 0
        for dim, count in enumerate(self.sizes):
            for step in range(1, count):
                target = list(self.at)
                target[dim] = lax.rem(self.at[dim] + step, count)
                pl.semaphore_signal(sem, inc=1, device_id=tuple(target), device_id_type=MESH)
                total += 1
        pl.semaphore_wait(sem, total)

    def faces(self):
        found = []
        for dim, count in enumerate(self.sizes):
            for side in (-1, 1):
                there = self.at[dim] > 0 if side < 0 else self.at[dim] < count - 1
                target = list(self.at)
                target[dim] = jnp.clip(self.at[dim] + side, 0, count - 1)
                found.append((there, tuple(target)))
        return found


AXES = ("y", "c", "gy", "gz")
ORDERS = (("c", "gz", "y", "gy"), ("c", "y", "gz", "gy"))


def select(fixed, rows, columns=slice(None)):
    return tuple(fixed.get(axis, slice(None)) for axis in AXES) + (rows, columns)


def stage_plan(sizes):
    gx, gy, gz = sizes
    counts = {"y": gx // 2, "c": 2, "gy": gy, "gz": gz}
    plan = []
    for half, order in enumerate(ORDERS):
        done = []
        for axis in order:
            done.append(axis)
            left = tuple(counts[a] for a in AXES if a not in done)
            plan.append((half, axis, counts[axis], left))
    return counts, plan


def scatter_scratch(sizes, width):
    counts, plan = stage_plan(sizes)
    rows = PIECE // 2
    shapes = [pltpu.VMEM((n - 1,) + left + (rows, width), BF16) for _, _, n, left in plan]
    copies = sum(n - 1 for _, _, n, _ in plan)
    work = pltpu.VMEM((counts["y"], 2, counts["gy"], counts["gz"], PIECE, width), BF16)
    return shapes + [work, pltpu.SemaphoreType.DMA((copies,)), pltpu.SemaphoreType.DMA((copies,))]


class Scatter:
    def __init__(self, place, source, scratch, columns=slice(None)):
        self.place = place
        self.columns = columns
        self.source = source
        self.recv = scratch[:8]
        self.work, self.send_sem, self.recv_sem = scratch[8:11]
        self.plan = stage_plan(place.sizes)[1]
        self.offsets = []
        total = 0
        for _, _, n, _ in self.plan:
            self.offsets.append(total)
            total += n - 1

    def rows(self, half):
        return pl.ds(half * (PIECE // 2), PIECE // 2)

    def fixed(self, half, level):
        return {axis: self.place.pos[axis] for axis in ORDERS[half][:level]}

    def copies(self, half, level):
        at = half * 4 + level
        axis, n = self.plan[at][1], self.plan[at][2]
        origin = self.source if level == 0 else self.work
        columns = self.columns if level == 0 else slice(None)
        found = []
        for step in range(1, n):
            target = lax.rem(self.place.pos[axis] + step, n)
            fixed = self.fixed(half, level)
            fixed[axis] = target
            found.append(
                pltpu.make_async_remote_copy(
                    src_ref=origin.at[select(fixed, self.rows(half), columns)],
                    dst_ref=self.recv[at].at[step - 1],
                    send_sem=self.send_sem.at[self.offsets[at] + step - 1],
                    recv_sem=self.recv_sem.at[self.offsets[at] + step - 1],
                    device_id=self.place.device(axis, target),
                    device_id_type=MESH,
                )
            )
        return found

    def start(self, level, halves=(0, 1)):
        for half in halves:
            for copy in self.copies(half, level):
                copy.start()

    def finish(self, level, out=None, halves=(0, 1)):
        for half in halves:
            at = half * 4 + level
            for copy in self.copies(half, level):
                copy.wait()
            origin = self.source if level == 0 else self.work
            where = select(self.fixed(half, level + 1), self.rows(half))
            taken = where[:-1] + ((self.columns if level == 0 else slice(None)),)
            total = origin[taken].astype(F32)
            for step in range(self.plan[at][2] - 1):
                total = total + self.recv[at][step].astype(F32)
            if out is None:
                self.work[where] = total.astype(BF16)
            else:
                out[self.rows(half), self.columns] = total.astype(out.dtype)

    def advance(self, level, halves=(0, 1)):
        for half in halves:
            self.finish(level, None, (half,))
            self.start(level + 1, (half,))


def gather_copies(place, final, send_sem, recv_sem, level, group, half, columns):
    counts, plan = stage_plan(place.sizes)
    order = ORDERS[half]
    axis = order[level]
    base = sum(n - 1 for _, _, n, _ in plan[: half * 4 + level])
    base += group * sum(n - 1 for _, _, n, _ in plan)
    fixed = {a: place.pos[a] for a in order[: level + 1]}
    view = final.at[select(fixed, pl.ds(half * (PIECE // 2), PIECE // 2), columns)]
    found = []
    for step in range(1, counts[axis]):
        target = lax.rem(place.pos[axis] + step, counts[axis])
        found.append(
            pltpu.make_async_remote_copy(
                src_ref=view,
                dst_ref=view,
                send_sem=send_sem.at[base + step - 1],
                recv_sem=recv_sem.at[base + step - 1],
                device_id=place.device(axis, target),
                device_id_type=MESH,
            )
        )
    return found


def groups_of(width):
    return 2 if width % (2 * LANES) == 0 else 1


def project_kernel(sizes, rows_ref, bias_ref, wq, wkv, wo, gin, baf, q_out, g_out, keys, final,
                   *scratch):
    width = baf.shape[-1]
    groups = groups_of(width)
    gs, gr, hs, hr = scratch[11 * groups :]
    place = Place(sizes)
    place.barrier()
    columns = [slice(g * (width // groups), (g + 1) * (width // groups)) for g in range(groups)]
    scatters = [
        Scatter(place, baf, scratch[11 * g : 11 * g + 11], columns[g]) for g in range(groups)
    ]
    for scatter in scatters:
        scatter.start(0)
    normed_low = layer_norm(rows_ref[...].astype(F32))[0].astype(BF16)
    keys[0:P_SIZE, 0 : 2 * D] = nn(normed_low, wkv[...]).astype(BF16)
    keys[0:P_SIZE, 2 * D : AUG] = bias_ref[...]
    faces = place.faces()

    def face_copy(face, slot):
        return pltpu.make_async_remote_copy(
            src_ref=keys.at[pl.ds(0, P_SIZE)],
            dst_ref=keys.at[pl.ds((1 + slot) * P_SIZE, P_SIZE)],
            send_sem=hs.at[face],
            recv_sem=hr.at[slot],
            device_id=faces[face][1],
            device_id_type=MESH,
        )

    for scatter in scatters:
        scatter.advance(0)

    def send_faces(wanted):
        for face in wanted:
            @pl.when(faces[face][0])
            def _(face=face):
                face_copy(face, face ^ 1).start()

            @pl.when(jnp.logical_not(faces[face][0]))
            def _(face=face):
                keys[(1 + face) * P_SIZE : (2 + face) * P_SIZE, :] = jnp.zeros((P_SIZE, AUG), BF16)

    send_faces((2, 3))
    q_out[...] = nn(normed_low, wq[...]).astype(BF16)
    g_out[...] = nt(gin[...], wo[...]).astype(BF16)
    for level in (1, 2):
        for scatter in scatters:
            scatter.advance(level)
    send_faces((0, 1, 4, 5))
    mine = final.at[place.pos["y"], place.pos["c"], place.pos["gy"], place.pos["gz"]]
    streams = [(g, half) for g in range(groups) for half in range(2)]

    def spread_copies(level, g, half):
        return gather_copies(place, final, gs, gr, level, g, half, columns[g])

    for g, half in streams:
        scatters[g].finish(3, mine, (half,))
        for copy in spread_copies(3, g, half):
            copy.start()
    for level in (3, 2, 1, 0):
        for g, half in streams:
            for copy in spread_copies(level, g, half):
                copy.wait()
            if level > 0:
                for copy in spread_copies(level - 1, g, half):
                    copy.start()
    for face, (there, _) in enumerate(faces):
        @pl.when(there)
        def _(face=face):
            face_copy(face, face ^ 1).wait_send()
            face_copy(face, face).wait_recv()


def attend_kernel(flags, count, q_ref, g_ref, k_ref, v_ref, b_ref, bk_ref, bv_ref, wo_ref,
                  update_ref, attn_ref, gq_ref, dk_ref, dv_ref, dbk_ref, dbv_ref, e_scr, p_scr, u_scr):
    lane = lax.broadcasted_iota(jnp.int32, (P_SIZE, PAIR), 1)
    zero = jnp.zeros((P_SIZE, PAIR), BF16)
    q = q_ref[...] * jnp.asarray(1.0 / math.sqrt(HD), BF16)
    g = g_ref[...]
    qcat = jnp.concatenate([jnp.where(lane < HD, q, zero), jnp.where(lane < HD, zero, q)], axis=0)
    gcat = jnp.concatenate([jnp.where(lane < HD, g, zero), jnp.where(lane < HD, zero, g)], axis=0)
    first = (lax.broadcasted_iota(jnp.int32, (2 * P_SIZE, LANES), 1) == 0).astype(BF16)
    qaug = jnp.concatenate([qcat, first], axis=1)
    chunks = ALL // P_SIZE

    def part(c):
        if c < 7:
            return slice(c * P_SIZE, (c + 1) * P_SIZE), k_ref, v_ref, dk_ref, dv_ref
        return slice((c - 7) * P_SIZE, (c - 6) * P_SIZE), bk_ref, bv_ref, dbk_ref, dbv_ref

    top = jnp.full((8, 2 * P_SIZE), -3e38, F32)
    for c in range(chunks):
        rows, keys = part(c)[:2]
        if c < 7:
            bias = b_ref[rows, :]
            if c > 0:
                bias = jnp.where(flags[c - 1] == 1, bias, jnp.asarray(masked_bias, BF16))
            scores = nt(jnp.concatenate([keys[rows, :], bias], axis=1), qaug)
        else:
            scores = nt(keys[rows, :], qcat)
        e_scr[c * P_SIZE : (c + 1) * P_SIZE, :] = scores
        top = jnp.maximum(top, jnp.max(scores.reshape(P_SIZE // 8, 8, 2 * P_SIZE), axis=0))
    top = jnp.max(top, axis=0, keepdims=True)
    total = jnp.zeros((8, 2 * P_SIZE), F32)
    for c in range(chunks):
        span = slice(c * P_SIZE, (c + 1) * P_SIZE)
        e = jnp.exp(e_scr[span, :] - top)
        e_scr[span, :] = e
        total = total + jnp.sum(e.reshape(P_SIZE // 8, 8, 2 * P_SIZE), axis=0)
    inverse = 1.0 / jnp.sum(total, axis=0, keepdims=True)
    attn_t = jnp.zeros((PAIR, 2 * P_SIZE), F32)
    for c in range(chunks):
        span = slice(c * P_SIZE, (c + 1) * P_SIZE)
        rows, _, values = part(c)[:3]
        p = (e_scr[span, :] * inverse).astype(BF16)
        p_scr[span, :] = p
        attn_t = attn_t + tn(values[rows, :], p)
    picked = jnp.concatenate([attn_t[:HD, :P_SIZE], attn_t[HD:, P_SIZE:]], axis=0)
    attn = picked.T.astype(BF16)
    attn_ref[...] = attn
    step = pl.program_id(0)
    projected = nn(attn, wo_ref[...])

    @pl.when(step == 0)
    def _():
        u_scr[...] = projected

    @pl.when(step > 0)
    def _():
        u_scr[...] += projected

    @pl.when(step == D // PAIR - 1)
    def _():
        slot = lax.broadcasted_iota(jnp.int32, (P_SIZE, D), 0)
        update_ref[...] = jnp.where(slot < count[0], u_scr[...], 0.0).astype(BF16)

    product = g.astype(F32).T * picked.astype(BF16).astype(F32)
    row_dot = jnp.concatenate(
        [
            jnp.sum(product[:HD], axis=0, keepdims=True),
            jnp.sum(product[HD:], axis=0, keepdims=True),
        ],
        axis=1,
    )
    gq_t = jnp.zeros((PAIR, 2 * P_SIZE), F32)
    for c in range(chunks):
        span = slice(c * P_SIZE, (c + 1) * P_SIZE)
        rows, keys, values, dkeys, dvalues = part(c)
        grad_prob = nt(values[rows, :], gcat)
        ds = (e_scr[span, :] * inverse * (grad_prob - row_dot)).astype(BF16)
        gq_t = gq_t + tn(keys[rows, :], ds)
        dkeys[rows, :] = nn(ds, qcat).astype(BF16)
        dvalues[rows, :] = nn(p_scr[span, :], gcat).astype(BF16)
    picked_q = jnp.concatenate([gq_t[:HD, :P_SIZE], gq_t[HD:, P_SIZE:]], axis=0)
    gq_ref[...] = (picked_q.T * (1.0 / math.sqrt(HD))).astype(BF16)


def return_kernel(sizes, rows_ref, wq, wkv, gin, attn, gq, dk, dv, base,
                  grad_out, wkv_out, wqo_out, base_out, rk, rv, *scratch):
    scatter_refs, (ss, rs) = scratch[:11], scratch[11:]
    place = Place(sizes)
    place.barrier()
    faces = place.faces()

    def face_copy(face, slot, which):
        source, target = ((dk, rk), (dv, rv))[which]
        return pltpu.make_async_remote_copy(
            src_ref=source.at[pl.ds((1 + face) * P_SIZE, P_SIZE)],
            dst_ref=target.at[slot],
            send_sem=ss.at[2 * face + which],
            recv_sem=rs.at[2 * slot + which],
            device_id=faces[face][1],
            device_id_type=MESH,
        )

    for face, (there, _) in enumerate(faces):
        @pl.when(there)
        def _(face=face):
            face_copy(face, face ^ 1, 0).start()
            face_copy(face, face ^ 1, 1).start()

        @pl.when(jnp.logical_not(there))
        def _(face=face):
            rk[face] = jnp.zeros((P_SIZE, D), BF16)
            rv[face] = jnp.zeros((P_SIZE, D), BF16)

    scatter = Scatter(place, base, scatter_refs)
    scatter.start(0)
    normed, inv_std = layer_norm(rows_ref[...].astype(F32))
    normed_low = normed.astype(BF16)
    wqo_out[:, :D] = tn(normed_low, gq[...]).astype(BF16)
    wqo_out[:, D:] = tn(attn[...], gin[...]).astype(BF16)
    scatter.finish(0)
    scatter.start(1)
    for face, (there, _) in enumerate(faces):
        @pl.when(there)
        def _(face=face):
            for which in range(2):
                face_copy(face, face ^ 1, which).wait_send()
                face_copy(face, face, which).wait_recv()
    scatter.finish(1)
    scatter.start(2)
    sum_k = dk[0:P_SIZE, :].astype(F32)
    sum_v = dv[0:P_SIZE, :].astype(F32)
    for face in range(6):
        sum_k = sum_k + rk[face].astype(F32)
        sum_v = sum_v + rv[face].astype(F32)
    pair_k = sum_k.astype(BF16)
    pair_v = sum_v.astype(BF16)
    wkv_out[:, :D] = tn(normed_low, pair_k).astype(BF16)
    wkv_out[:, D:] = tn(normed_low, pair_v).astype(BF16)
    scatter.finish(2)
    scatter.start(3)
    grad = nt(gq[...], wq[...]) + nt(pair_k, wkv[:, :D]) + nt(pair_v, wkv[:, D:])
    first_mean = jnp.mean(grad, axis=-1, keepdims=True)
    second_mean = jnp.mean(grad * normed, axis=-1, keepdims=True)
    grad_out[...] = (inv_std * (grad - first_mean - normed * second_mean)).astype(BF16)
    scatter.finish(3, base_out)


def scatter_kernel(sizes, source, out, *scratch):
    place = Place(sizes)
    place.barrier()
    scatter = Scatter(place, source, scratch)
    for level in range(4):
        scatter.start(level)
        scatter.finish(level, out if level == 3 else None)


def finish_kernel(sizes, rows_ref, wq, wkv, gin, attn, gq, dk, dv, dbk, dbv,
                  grad_out, base_out, sum_out, rk, rv, base, weights, *scratch):
    base_refs, weight_refs, (ss, rs) = scratch[:11], scratch[11:22], scratch[22:]
    gx, gy, gz = sizes
    devices = gx * gy * gz
    half = PIECE // 2
    place = Place(sizes)
    place.barrier()
    faces = place.faces()

    def spread(target, rows, columns, values):
        step = values.shape[0] // devices
        for d in range(devices):
            x, y, z = d // (gy * gz), d // gz % gy, d % gz
            target[x // 2, x % 2, y, z, rows, columns] = values[d * step : (d + 1) * step]

    def face_copy(face, slot, which):
        source, target = ((dk, rk), (dv, rv))[which]
        return pltpu.make_async_remote_copy(
            src_ref=source.at[pl.ds((1 + face) * P_SIZE, P_SIZE)],
            dst_ref=target.at[slot],
            send_sem=ss.at[2 * face + which],
            recv_sem=rs.at[2 * slot + which],
            device_id=faces[face][1],
            device_id_type=MESH,
        )

    for face, (there, _) in enumerate(faces):
        @pl.when(there)
        def _(face=face):
            face_copy(face, face ^ 1, 0).start()
            face_copy(face, face ^ 1, 1).start()

        @pl.when(jnp.logical_not(there))
        def _(face=face):
            rk[face] = jnp.zeros((P_SIZE, D), BF16)
            rv[face] = jnp.zeros((P_SIZE, D), BF16)

    both, lower, upper = slice(0, PIECE), slice(0, half), slice(half, PIECE)
    left, right = slice(0, D), slice(D, 2 * D)
    spread(base, both, left, dbk[...])
    spread(base, both, right, dbv[...])
    first = Scatter(place, base, base_refs)
    second = Scatter(place, weights, weight_refs)
    first.start(0)
    normed, inv_std = layer_norm(rows_ref[...].astype(F32))
    normed_low = normed.astype(BF16)
    spread(weights, upper, left, tn(normed_low, gq[...]).astype(BF16))
    spread(weights, upper, right, tn(attn[...], gin[...]).astype(BF16))
    second.start(0, (1,))
    first.advance(0)
    second.advance(0, (1,))
    first.advance(1)
    for face, (there, _) in enumerate(faces):
        @pl.when(there)
        def _(face=face):
            for which in range(2):
                face_copy(face, face ^ 1, which).wait_send()
                face_copy(face, face, which).wait_recv()
    sum_k = dk[0:P_SIZE, :].astype(F32)
    sum_v = dv[0:P_SIZE, :].astype(F32)
    for face in range(6):
        sum_k = sum_k + rk[face].astype(F32)
        sum_v = sum_v + rv[face].astype(F32)
    pair_k = sum_k.astype(BF16)
    pair_v = sum_v.astype(BF16)
    spread(weights, lower, left, tn(normed_low, pair_k).astype(BF16))
    spread(weights, lower, right, tn(normed_low, pair_v).astype(BF16))
    second.start(0, (0,))
    second.advance(1, (1,))
    second.advance(0, (0,))
    grad = nt(gq[...], wq[...]) + nt(pair_k, wkv[:, :D]) + nt(pair_v, wkv[:, D:])
    first_mean = jnp.mean(grad, axis=-1, keepdims=True)
    second_mean = jnp.mean(grad * normed, axis=-1, keepdims=True)
    grad_out[...] = (inv_std * (grad - first_mean - normed * second_mean)).astype(BF16)
    first.advance(2)
    second.advance(2, (1,))
    second.advance(1, (0,))
    first.finish(3, base_out)
    second.finish(3, sum_out, (1,))
    second.advance(2, (0,))
    second.finish(3, sum_out, (0,))


def vmem():
    return pl.BlockSpec(memory_space=pltpu.VMEM)


def shape(dims, dtype):
    return jax.ShapeDtypeStruct(dims, dtype)


def remote(kernel, sizes, outs, scratch, collective, operands):
    return pl.pallas_call(
        functools.partial(kernel, sizes),
        out_shape=outs,
        in_specs=[vmem()] * len(operands),
        out_specs=jax.tree.map(lambda _: vmem(), outs),
        scratch_shapes=scratch,
        compiler_params=pltpu.CompilerParams(
            collective_id=collective, has_side_effects=True, vmem_limit_bytes=VMEM_BYTES
        ),
    )(*operands)


def attend(flags, count, q, g, keys, baffle, output_weight):
    def cols(rows, shift):
        return pl.BlockSpec((rows, PAIR), lambda p: (0, p + shift))

    groups = D // PAIR
    return pl.pallas_call(
        attend_kernel,
        grid=(groups,),
        out_shape=(
            shape((P_SIZE, D), BF16),
            shape((P_SIZE, D), BF16),
            shape((P_SIZE, D), BF16),
            shape((NEAR, D), BF16),
            shape((NEAR, D), BF16),
            shape((NB, D), BF16),
            shape((NB, D), BF16),
        ),
        in_specs=[
            pl.BlockSpec(memory_space=pltpu.SMEM),
            pl.BlockSpec(memory_space=pltpu.SMEM),
            cols(P_SIZE, 0),
            cols(P_SIZE, 0),
            cols(NEAR, 0),
            cols(NEAR, groups),
            pl.BlockSpec((NEAR, PAIR), lambda p: (0, 2 * groups)),
            cols(NB, 0),
            cols(NB, groups),
            pl.BlockSpec((PAIR, D), lambda p: (p, 0)),
        ],
        out_specs=(
            pl.BlockSpec((P_SIZE, D), lambda p: (0, 0)),
            cols(P_SIZE, 0),
            cols(P_SIZE, 0),
            cols(NEAR, 0),
            cols(NEAR, 0),
            cols(NB, 0),
            cols(NB, 0),
        ),
        scratch_shapes=[
            pltpu.VMEM((ALL, 2 * P_SIZE), F32),
            pltpu.VMEM((ALL, 2 * P_SIZE), BF16),
            pltpu.VMEM((P_SIZE, D), F32),
        ],
        compiler_params=pltpu.CompilerParams(vmem_limit_bytes=VMEM_BYTES),
    )(flags, count, q, g, keys, keys, keys, baffle, baffle, output_weight)


def body(
    sizes,
    particles,
    log_weight,
    counts,
    pattern,
    query_weight,
    key_value_weight,
    output_weight,
    baffle_store,
    owner_device,
    cotangent,
):
    gx, gy, gz = sizes
    devices = gx * gy * gz
    rows_in = particles[0, 0, 0]
    valid_rows = jnp.arange(P_SIZE, dtype=jnp.int32) < counts[0, 0, 0]
    own_bias = jnp.where(valid_rows, log_weight[0, 0, 0], jnp.asarray(masked_bias, BF16))
    bias_lanes = jnp.broadcast_to(own_bias[:, None], (P_SIZE, LANES))
    grad_in = jnp.where(valid_rows[:, None], cotangent[0, 0, 0], jnp.zeros((), BF16))
    me = lax.axis_index(("gx", "gy", "gz"))
    width = NB * 2 * D // (devices * PIECE)
    pieces = (gx // 2, 2, gy, gz, PIECE, width)
    store = jnp.where(me == owner_device[0], baffle_store[0], jnp.zeros((), BF16)).reshape(pieces)
    groups = groups_of(width)
    copies = groups * sum(n - 1 for _, _, n, _ in stage_plan(sizes)[1])
    dma = pltpu.SemaphoreType.DMA
    q, g, keys, final = remote(
        project_kernel,
        sizes,
        (
            shape((P_SIZE, D), BF16),
            shape((P_SIZE, D), BF16),
            shape((NEAR, AUG), BF16),
            shape(pieces, BF16),
        ),
        scatter_scratch(sizes, width // groups) * groups
        + [dma((copies,)), dma((copies,)), dma((6,)), dma((6,))],
        0,
        (rows_in, bias_lanes, query_weight, key_value_weight, output_weight, grad_in, store),
    )
    baffle = final.reshape(NB, 2 * D)
    update, attn, gq, dk, dv, dbk, dbv = attend(
        pattern[0, 0, 0], counts[0, 0], q, g, keys, baffle, output_weight
    )
    halos = [pltpu.VMEM((6, P_SIZE, D), BF16), pltpu.VMEM((6, P_SIZE, D), BF16)]
    face_sems = [dma((12,)), dma((12,))]
    if width == 2 * D:
        half = PIECE // 2
        grad_rows, base_sum, weight_sum = remote(
            finish_kernel,
            sizes,
            (
                shape((P_SIZE, D), BF16),
                shape((PIECE, width), F32),
                shape((PIECE, width), F32),
            ),
            halos
            + [pltpu.VMEM(pieces, BF16), pltpu.VMEM(pieces, BF16)]
            + scatter_scratch(sizes, width)
            + scatter_scratch(sizes, width)
            + face_sems,
            1,
            (
                rows_in,
                query_weight,
                key_value_weight,
                grad_in,
                attn,
                gq,
                dk,
                dv,
                dbk,
                dbv,
            ),
        )
        grad_kv = weight_sum[:half].reshape(-1)
        grad_q = weight_sum[half:, :D].reshape(-1)
        grad_o = weight_sum[half:, D:].reshape(-1)
    else:
        base = jnp.concatenate([dbk, dbv], axis=1).reshape(pieces)
        grad_rows, w_kv, w_qo, base_sum = remote(
            return_kernel,
            sizes,
            (
                shape((P_SIZE, D), BF16),
                shape((D, 2 * D), BF16),
                shape((D, 2 * D), BF16),
                shape((PIECE, width), F32),
            ),
            halos + scatter_scratch(sizes, width) + face_sems,
            2,
            (rows_in, query_weight, key_value_weight, grad_in, attn, gq, dk, dv, base),
        )
        weights = jnp.concatenate(
            [
                w_kv.reshape(devices, -1),
                w_qo[:, :D].reshape(devices, -1),
                w_qo[:, D:].reshape(devices, -1),
            ],
            axis=1,
        )
        weight_sum = remote(
            scatter_kernel,
            sizes,
            shape((PIECE, width), F32),
            scatter_scratch(sizes, width),
            3,
            (weights.reshape(pieces),),
        )
        flat = weight_sum.reshape(-1)
        part = D * D // devices
        grad_kv, grad_q, grad_o = flat[: 2 * part], flat[2 * part : 3 * part], flat[3 * part :]
    return (
        update[None, None, None],
        grad_rows[None, None, None],
        grad_q,
        grad_kv,
        grad_o,
        base_sum.reshape(-1),
    )


def solution(mesh):
    sizes = tuple(mesh.shape[axis] for axis in ("gx", "gy", "gz"))
    return jax.shard_map(
        functools.partial(body, sizes),
        mesh=mesh,
        in_specs=(
            P("gx", "gy", "gz", None, None),
            P("gx", "gy", "gz", None),
            P("gx", "gy", "gz"),
            P("gx", "gy", "gz", None),
            P(),
            P(),
            P(),
            P(("gx", "gy", "gz"), None, None),
            P(),
            P("gx", "gy", "gz", None, None),
        ),
        out_specs=(
            P("gx", "gy", "gz", None, None),
            P("gx", "gy", "gz", None, None),
            P(("gx", "gy", "gz")),
            P(("gx", "gy", "gz")),
            P(("gx", "gy", "gz")),
            P(("gx", "gy", "gz")),
        ),
        check_vma=False,
    )
```
